128 devices in a mesh: pipe: 4 (over y), dp: 32 (over z, x, core).
Axes of the slice: x: 4, y: 4, z: 4, core: 2. Of those that a mesh axis runs over, the one named last changes fastest.
Arguments:
- cotangent: bfloat16 [2, 128, 4096], P(None, None, 'dp'), may hold values from -4 to 4
- stashed_inputs: bfloat16 [4, 2, 128, 4096], P('pipe', None, None, 'dp'), may hold values from -4 to 4
- weights: bfloat16 [4, 4096, 4096], P('pipe', 'dp'), may hold values from -0.09375 to 0.09375
- momentum: bfloat16 [4, 4096, 4096], P('pipe', 'dp'), may hold values from -560 to 560
Outputs:
- input_grads: bfloat16 [4, 2, 128, 4096], P('pipe', None, None, 'dp')
- new_momentum: bfloat16 [4, 4096, 4096], P('pipe', 'dp')
- orth_update: bfloat16 [4, 4096, 4096], P('pipe', 'dp')
The draws below stay inside these ranges and needn't reach their ends.
All inputs are finite; a program needn't handle non-finite values.
Results may differ from the reference program's by a relative error of at most 0.008.
Values may be sent and summed in bfloat16 or wider, within the bound.
A program may use at most 192 MiB of HBM per device.

```python
import math
import jax
import jax.numpy as jnp

D = 4096
TOK = 128
MB = 2
LAYERS = 4


def bounded_base(key_base, full_shape):
    return jnp.clip(jax.random.normal(key_base, full_shape, jnp.float32), -4.0, 4.0)


def draw_cotangent(key, part):
    return bounded_base(jax.random.fold_in(key, 11), (MB, TOK, D)).astype(jnp.bfloat16)


def draw_stashed_inputs(key, part):
    return bounded_base(jax.random.fold_in(key, 12), (LAYERS, MB, TOK, D)).astype(jnp.bfloat16)


def draw_momentum(key, part):
    key_base = jax.random.fold_in(key, 21)
    key_rows = jax.random.fold_in(key, 22)
    key_cols = jax.random.fold_in(key, 23)
    base_vals = bounded_base(key_base, (LAYERS, D, D))
    trend = 2.0
    row_pos = jnp.arange(D, dtype=jnp.float32) / float(D - 1)
    row_trend = jnp.sqrt(1.0 + trend * row_pos)[None, :, None]
    row_spread = jnp.exp(1.1512925 * jax.random.uniform(key_rows, (LAYERS, D, 1), jnp.float32))
    col_spread = jnp.exp(1.1512925 * jax.random.uniform(key_cols, (LAYERS, 1, D), jnp.float32))
    return (8.0 * base_vals * row_trend * row_spread * col_spread).astype(jnp.bfloat16)


def block_scale(stream_key, shape, pieces, least, high):
    loudness = 1.0
    for axis_at, blocks in pieces:
        steps = jax.random.uniform(jax.random.fold_in(jax.random.fold_in(stream_key, 6), axis_at), (blocks,), jnp.float32, least / len(pieces), high / len(pieces))
        loudness = loudness * jnp.repeat(jnp.exp(steps), shape[axis_at] // blocks).reshape((-1,) + (1,) * (len(shape) - 1 - axis_at))
    return loudness


def normal_values(key, shape, scale, bound, cuts=(), kind=jnp.bfloat16):
    loudness = block_scale(key, shape, cuts, -0.22, 0.18) if cuts else 1.0
    result = jax.random.normal(key, shape, jnp.float32) * scale * loudness
    return jnp.minimum(jnp.maximum(result, -bound), bound).astype(kind)


def setup_inputs(seed: int = 0) -> dict:
    key_of = jax.random.split(jax.random.key(seed), 5)
    return {
        "cotangent": draw_cotangent(jax.random.fold_in(key_of[4], 71), 0),
        "stashed_inputs": draw_stashed_inputs(jax.random.fold_in(key_of[4], 71), 0),
        "weights": normal_values(key_of[2], (LAYERS, D, D), D ** -0.5, 0.09375, ((0, 4), (1, 32))),
        "momentum": draw_momentum(jax.random.fold_in(key_of[4], 71), 0),
    }


quintic_a = 3.4445
quintic_b = -4.775
quintic_c = 2.0315

def newton_step(fresh_moment):
    fresh32 = fresh_moment.astype(jnp.float32)
    sum_squares = jnp.sum(fresh32 * fresh32)
    scaling = 0.4 / jnp.sqrt(D * (sum_squares / (float(D) * float(D)) + 1e-06))
    matrix_x = (fresh32 * scaling).astype(jnp.bfloat16)
    gram_full = jnp.dot(matrix_x, matrix_x.T, preferred_element_type=jnp.float32).astype(jnp.bfloat16)
    cubic_full = jnp.dot(gram_full, matrix_x, preferred_element_type=jnp.float32).astype(jnp.bfloat16)
    back_full = jnp.dot(cubic_full, matrix_x.T, preferred_element_type=jnp.float32).astype(jnp.bfloat16)
    quintic_full = jnp.dot(back_full, matrix_x, preferred_element_type=jnp.float32)
    mixed = quintic_a * matrix_x.astype(jnp.float32) + quintic_b * cubic_full.astype(jnp.float32) + quintic_c * quintic_full
    return (math.sqrt(D) * mixed).astype(jnp.bfloat16)

def reference(cotangent, stashed_inputs, weights, momentum):
    upstream = cotangent
    grads_list = [None] * LAYERS
    moment_list = [None] * LAYERS
    update_list = [None] * LAYERS
    for section in reversed(range(LAYERS)):
        inputs = stashed_inputs[section].astype(jnp.float32)
        flat_up = upstream.reshape(MB * TOK, D)
        back_proj = jnp.dot(flat_up, weights[section].T, preferred_element_type=jnp.float32).reshape(MB, TOK, D)
        sigmoid_val = jax.nn.sigmoid(inputs)
        slopes = sigmoid_val * (1.0 + inputs * (1.0 - sigmoid_val))
        dinput = (upstream.astype(jnp.float32) + slopes * back_proj).astype(jnp.bfloat16)
        gated_acts = (inputs * sigmoid_val).astype(jnp.bfloat16).reshape(MB * TOK, D)
        weight_grad = jnp.dot(gated_acts.T, flat_up, preferred_element_type=jnp.float32)
        fresh_moment = (0.95 * momentum[section].astype(jnp.float32) + weight_grad).astype(jnp.bfloat16)
        grads_list[section] = dinput
        moment_list[section] = fresh_moment
        update_list[section] = newton_step(fresh_moment)
        upstream = dinput
    return (jnp.stack(grads_list), jnp.stack(moment_list), jnp.stack(update_list))
```

```python
import functools
import math

import jax
import jax.numpy as jnp
from jax import lax
from jax.experimental import pallas as pl
from jax.experimental.pallas import tpu as pltpu
from jax.sharding import PartitionSpec as P

quintic_a = 3.4445
quintic_b = -4.775
quintic_c = 2.0315

MESH = pl.DeviceIdType.MESH
BF = jnp.bfloat16
F32 = jnp.float32
RING = 4
CHIPS = 16
LANE = 128
WIDTH = 4096
HALF = 2048
TOKENS = 256
ROWS = 256
NT = (((1,), (1,)), ((), ()))
NN = (((1,), (0,)), ((), ()))


def place():
    spot = lax.axis_index("dp")
    return lax.axis_index("pipe"), spot // 8, (spot // 2) % RING, spot % 2


def at(y, z, x, core):
    return (y, ((z % RING) * RING + x % RING) * 2 + core)


def chip_of(z, x):
    return (z % RING) * RING + x % RING


def multiple(value, of):
    return pl.multiple_of(value, of)


def offset_of(index):
    return index + (index // 2) * (5 - 2 * index)


class Gather:
    def __init__(self, slot, send, recv):
        self.slot, self.send, self.recv = slot, send, recv
        self.y, self.z, self.x, self.core = place()

    def block(self, part, first, second):
        if part == 0:
            return chip_of(self.z + second, self.x + first)
        return chip_of(self.z + first, self.x + second)

    def target(self, part, axis, steps):
        along_x = (axis == 0) == (part == 0)
        if along_x:
            return at(self.y, self.z, self.x + steps, self.core)
        return at(self.y, self.z + steps, self.x, self.core)

    def copy(self, part, first, second, half, axis, steps, number):
        block = self.block(part, first, second)
        ref = self.slot(block, part, half)
        return pltpu.make_async_remote_copy(
            src_ref=ref,
            dst_ref=ref,
            send_sem=self.send.at[number],
            recv_sem=self.recv.at[block, part, half],
            device_id=self.target(part, axis, steps),
            device_id_type=MESH,
        )

    def put(self, part, first, second, half, axis, steps, number):
        self.copy(part, first, second, half, axis, steps, number).start()

    def wait(self, part, first, second, half):
        self.copy(part, first, second, half, 0, 1, 0).wait_recv()

    def sent(self, number, part=0, half=0):
        self.copy(part, 0, 0, half, 0, 1, number).wait_send()


def step_kernel(
    cot, xs, w, m, dout, nout, oout,
    mbuf, nbuf, wbuf, ubuf, gbuf, xin, slope, dbuf, bsend, brecv, bown, apart, aother, fpart, fother,
    eacc, ebf, qacc, obuf, own_sum, other_sum, own_all, other_all,
    lsem, sib_send, sib_recv, msend, mrecv, gsend, grecv, usend, urecv,
    asend, arecv, fsend, frecv, osem, orecv, nsem, nrecv,
):
    y, z, x, core = place()
    me = chip_of(z, x)
    sibling = at(y, z, x, 1 - core)

    def remote(src, dst, send_sem, recv_sem, device=sibling):
        return pltpu.make_async_remote_copy(
            src_ref=src, dst_ref=dst, send_sem=send_sem, recv_sem=recv_sem,
            device_id=device, device_id_type=MESH,
        )

    partners = [at(y, z, x + 1, core), at(y, z, x + 2, core), at(y, z, x + 3, core),
                at(y, z + 1, x, core), at(y, z + 2, x, core), at(y, z + 3, x, core),
                sibling, at((y + 1) % RING, z, x, core), at((y + 3) % RING, z, x, core)]
    load_x = pltpu.make_async_copy(xs.at[0], xin, lsem.at[0])
    load_x.start()
    barrier = pltpu.get_barrier_semaphore()
    for partner in partners:
        pl.semaphore_signal(barrier, 1, device_id=partner, device_id_type=MESH)

    def row(core_at, height=LANE):
        return pl.ds(multiple(me * ROWS + core_at * LANE, LANE), height)

    def own_columns(k, core_at):
        return pl.ds(multiple((2 * k + core_at) * LANE, LANE), LANE)

    def load_own(k, carry):
        lanes = pl.ds(multiple(k * LANE, LANE), LANE)
        pltpu.make_async_copy(m.at[0, :, own_columns(k, core)], mbuf.at[row(core), lanes], lsem.at[1]).start()
        pltpu.make_async_copy(w.at[0, :, own_columns(k, core)], wbuf.at[core, :, lanes], lsem.at[2]).start()
        return carry

    lax.fori_loop(0, CHIPS, load_own, 0)
    pl.semaphore_wait(barrier, len(partners))

    def give_sibling(k, carry):
        lanes = pl.ds(multiple(k * LANE, LANE), LANE)
        remote(m.at[0, :, own_columns(k, 1 - core)], mbuf.at[row(core), lanes],
               sib_send.at[0], sib_recv.at[0]).start()
        remote(w.at[0, :, own_columns(k, 1 - core)], wbuf.at[core, :, lanes],
               sib_send.at[1], sib_recv.at[1]).start()
        return carry

    lax.fori_loop(0, CHIPS, give_sibling, 0)

    load_x.wait()
    values = xin[...].reshape(TOKENS, LANE).astype(F32)
    sigmoid_val = jax.nn.sigmoid(values)
    slope[...] = sigmoid_val * (1.0 + values * (1.0 - sigmoid_val))
    gated = (values * sigmoid_val).astype(BF).astype(F32)
    gbuf[core, pl.ds(multiple(me * LANE, LANE), LANE), :] = jnp.transpose(gated).astype(BF)

    def m_slot(block, part, half):
        return mbuf.at[pl.ds(multiple(block * ROWS + part * LANE + half * 64, 64), 64), :]

    def g_slot(block, part, half):
        return gbuf.at[core, pl.ds(multiple(block * LANE + part * 64 + half * 32, 32), 32), :]

    def u_slot(block, part, half):
        return ubuf.at[pl.ds(part * LANE, LANE), pl.ds(multiple(block * LANE, LANE), LANE)]

    bulk = [Gather(m_slot, msend, mrecv), Gather(g_slot, gsend, grecv)]
    few = Gather(u_slot, usend, urecv)

    def own_u():
        return ubuf.at[:, pl.ds(multiple(me * LANE, LANE), LANE)]

    def from_above():
        return remote(dbuf, own_u(), sib_send.at[3], sib_recv.at[3], at((y + 3) % RING, z, x, core))

    def chain():
        @pl.when(y == RING - 1)
        def _():
            for micro in range(2):
                pltpu.make_async_copy(
                    cot.at[micro],
                    ubuf.at[pl.ds(micro * LANE, LANE), pl.ds(multiple(me * LANE, LANE), LANE)],
                    lsem.at[3]).start()
            pltpu.make_async_copy(own_u(), own_u(), lsem.at[3]).wait()

        @pl.when(y < RING - 1)
        def _():
            from_above().wait_recv()

        number = 0
        for axis in (0, 1):
            for part in (0, 1):
                for steps in (1, 3, 2):
                    few.put(part, 0, 0, 0, axis, steps, number)
                    number += 1
        for first in (1, 3, 2):
            for part in (0, 1):
                few.wait(part, first, 0, 0)
                for steps in (1, 3, 2):
                    few.put(part, first, 0, 0, 1, steps, number)
                    number += 1
        for first in (0, 1, 3, 2):
            for part in (0, 1):
                for second in (1, 3, 2):
                    few.wait(part, first, second, 0)
        pltpu.make_async_copy(wbuf.at[core], wbuf.at[core], lsem.at[2]).wait()
        remote(wbuf.at[core], wbuf.at[core], sib_send.at[1], sib_recv.at[1]).wait_recv()
        full = ubuf[...]
        bsend[...] = lax.dot_general(full, wbuf[1 - core], NT, preferred_element_type=F32)
        give = remote(bsend, brecv, sib_send.at[2], sib_recv.at[2])
        give.start()
        bown[...] = lax.dot_general(full, wbuf[core], NT, preferred_element_type=F32)
        give.wait()
        back = bown[...] + brecv[...]
        upstream = ubuf[:, pl.ds(multiple(me * LANE, LANE), LANE)].astype(F32)
        dbuf[...] = (upstream + slope[...] * back).astype(BF)

        @pl.when(y > 0)
        def _():
            from_above().start()

        for micro in range(2):
            pltpu.make_async_copy(
                dbuf.at[pl.ds(micro * LANE, LANE), :], dout.at[0, micro], lsem.at[4]).start()

        @pl.when(y > 0)
        def _():
            from_above().wait_send()

    pltpu.make_async_copy(mbuf.at[row(core)], mbuf.at[row(core)], lsem.at[1]).wait()
    remote(mbuf.at[row(core)], mbuf.at[row(core)], sib_send.at[0], sib_recv.at[0]).wait_recv()

    def begin():
        for part in (0, 1):
            for half in (0, 1):
                for steps in (1, 3):
                    for one in bulk:
                        one.put(part, 0, 0, half, 0, steps, 48 + part * 4 + half * 2 + steps // 2)

    def phase(index):
        first = offset_of(index)

        @pl.when((index > 0) & (index < 4))
        def _():
            for part in (0, 1):
                for one in bulk:
                    one.wait(part, first, 0, 0)
                    one.wait(part, first, 0, 1)

        @pl.when(index == 1)
        def _():
            for part in (0, 1):
                for one in bulk:
                    one.put(part, 1, 0, 1, 0, 3, 56 + part * 2)

        @pl.when(index == 2)
        def _():
            for part in (0, 1):
                for one in bulk:
                    one.put(part, 3, 0, 0, 0, 1, 57 + part * 2)

        @pl.when(index < 4)
        def _():
            for part in (0, 1):
                for half in (0, 1):
                    for steps in (1, 3):
                        for one in bulk:
                            one.put(part, first, 0, half, 1, steps,
                                    index * 12 + part * 6 + half * 2 + steps // 2)

        @pl.when(index > 0)
        def _():
            before = offset_of(index - 1)
            for part in (0, 1):
                for one in bulk:
                    one.wait(part, before, 3, 0)
                    one.put(part, before, 3, 0, 1, 1, (index - 1) * 12 + part * 6 + 4)
                    one.wait(part, before, 1, 1)
                    one.put(part, before, 1, 1, 1, 3, (index - 1) * 12 + part * 6 + 5)

    begin()

    def phases(index, carry):
        @pl.when(index == RING - 1 - y)
        def _():
            chain()

        phase(index)
        return carry

    lax.fori_loop(0, RING + 1, phases, 0)

    def arrivals(index, carry):
        first = offset_of(index)
        for part in (0, 1):
            for one in bulk:
                one.wait(part, first, 3, 1)
                one.wait(part, first, 1, 0)
                one.wait(part, first, 2, 0)
                one.wait(part, first, 2, 1)
        return carry

    lax.fori_loop(0, RING, arrivals, 0)
    relay = remote(gbuf.at[core], gbuf.at[core], sib_send.at[4], sib_recv.at[4])
    relay.start()
    relay.wait_send()
    remote(gbuf.at[1 - core], gbuf.at[1 - core], sib_send.at[4], sib_recv.at[4]).wait_recv()

    def rows_of(block, height=ROWS):
        return pl.ds(multiple(block * ROWS, ROWS), height)

    def build(block, total):
        for part in (0, 1):
            where = pl.ds(multiple(block * ROWS + part * LANE, LANE), LANE)
            grad = lax.dot_general(
                gbuf[part, pl.ds(multiple(block * LANE, LANE), LANE), :], ubuf[...], NN,
                preferred_element_type=F32)
            fresh = (0.95 * mbuf[where, :].astype(F32) + grad).astype(BF)
            nbuf[where, :] = fresh
            wide = fresh.astype(F32)
            square = wide * wide
            total = total + jnp.sum(square.reshape(16, 8, 16, LANE), axis=(0, 2))
        return total

    zero = jnp.zeros((8, LANE), F32)
    total = build(me, zero)
    own_sum[...] = total
    swap = remote(own_sum, other_sum, sib_send.at[5], sib_recv.at[5])
    swap.start()
    def give_rows(buf, base, out, sem, recv):
        def body(k, carry):
            lanes = pl.ds(multiple(k * LANE, LANE), LANE)
            pltpu.make_async_copy(
                buf.at[pl.ds(multiple(base + core * LANE, LANE), LANE), lanes],
                out.at[0, :, own_columns(k, core)], sem.at[0]).start()
            remote(buf.at[pl.ds(multiple(base + (1 - core) * LANE, LANE), LANE), lanes],
                   out.at[0, :, own_columns(k, core)], sem.at[1], recv).start()
            return carry
        lax.fori_loop(0, CHIPS, body, 0)

    def wait_rows(buf, out, sem, recv):
        pltpu.make_async_copy(buf.at[pl.ds(0, LANE), :], buf.at[pl.ds(0, LANE), :], sem.at[0]).wait()
        both = remote(buf.at[pl.ds(0, LANE), :], buf.at[pl.ds(0, LANE), :], sem.at[1], recv)
        both.wait_send()
        both.wait_recv()

    give_rows(nbuf, me * ROWS, nout, nsem, nrecv)
    swap.wait()
    chip_norm = jnp.sqrt(jnp.maximum(jnp.sum(own_sum[...] + other_sum[...]), 1e-30))
    inverse = 1.0 / chip_norm

    def a_copy(block):
        return remote(apart.at[block], aother.at[block], asend.at[block], arecv.at[block])

    def f_copy(block):
        return remote(fpart.at[block], fother.at[block], fsend.at[block], frecv.at[block])

    def gram(block):
        part = lax.dot_general(nbuf[rows_of(me), :], nbuf[rows_of(block), :], NT,
                               preferred_element_type=F32)
        apart[block] = (part * inverse).astype(BF)
        a_copy(block).start()

    def cubic(block):
        a_copy(block).wait_recv()
        whole = (apart[block].astype(F32) + aother[block].astype(F32)).astype(BF)
        eacc[...] += lax.dot_general(whole, nbuf[rows_of(block), :], NN, preferred_element_type=F32)

    def turn(index):
        return (me + index) % CHIPS

    eacc[...] = jnp.zeros_like(eacc)
    gram(me)

    def stream(index, total):
        block = turn(index)
        total = build(block, total)
        gram(block)
        cubic(turn(index - 1))
        return total

    total = lax.fori_loop(1, CHIPS, stream, total)
    own_all[...] = total
    swap_all = remote(own_all, other_all, sib_send.at[6], sib_recv.at[6])
    swap_all.start()
    cubic(turn(CHIPS - 1))
    swap_all.wait()
    sum_squares = jnp.sum(own_all[...] + other_all[...])
    scaling = 0.4 / jnp.sqrt(float(WIDTH) * (sum_squares / float(WIDTH * WIDTH) + 1e-06))
    ebf[...] = (((eacc[...] * scaling) * scaling) * (scaling * chip_norm)).astype(BF)

    def back_part(block):
        part = lax.dot_general(ebf[...], nbuf[rows_of(block), :], NT, preferred_element_type=F32)
        fpart[block] = (part * scaling).astype(BF)
        f_copy(block).start()

    def quintic(block):
        f_copy(block).wait_recv()
        whole = (fpart[block].astype(F32) + fother[block].astype(F32)).astype(BF)
        qacc[...] += lax.dot_general(whole, nbuf[rows_of(block), :], NN, preferred_element_type=F32)

    qacc[...] = jnp.zeros_like(qacc)
    back_part(turn(0))
    back_part(turn(1))

    def tail(index, carry):
        back_part(turn(index))
        quintic(turn(index - 2))
        return carry

    lax.fori_loop(2, CHIPS, tail, 0)
    quintic(turn(CHIPS - 2))
    quintic(turn(CHIPS - 1))
    scaled = (nbuf[rows_of(me), :].astype(F32) * scaling).astype(BF).astype(F32)
    mixed = (quintic_a * scaled + quintic_b * ebf[...].astype(F32)
             + quintic_c * (qacc[...] * scaling))
    obuf[...] = (math.sqrt(WIDTH) * mixed).astype(BF)
    give_rows(obuf, 0, oout, osem, orecv)

    pltpu.make_async_copy(dbuf, dbuf, lsem.at[4]).wait()
    remote(mbuf.at[row(core)], mbuf.at[row(core)], sib_send.at[0], sib_recv.at[0]).wait_send()
    remote(wbuf.at[core], wbuf.at[core], sib_send.at[1], sib_recv.at[1]).wait_send()

    def drain_bulk(number, carry):
        for one in bulk:
            one.sent(number)
        return carry

    lax.fori_loop(0, 60, drain_bulk, 0)

    def drain_few(number, carry):
        few.sent(number)
        return carry

    lax.fori_loop(0, 30, drain_few, 0)

    def drain_pairs(block, carry):
        a_copy(block).wait_send()
        f_copy(block).wait_send()
        return carry

    lax.fori_loop(0, CHIPS, drain_pairs, 0)
    wait_rows(nbuf, nout, nsem, nrecv)
    wait_rows(obuf, oout, osem, orecv)


def per_device(cotangent, stashed_inputs, weights, momentum):
    anywhere = pl.BlockSpec(memory_space=pl.ANY)
    sem = pltpu.SemaphoreType.DMA
    scratch = [
        pltpu.VMEM((WIDTH, HALF), BF),
        pltpu.VMEM((WIDTH, HALF), BF),
        pltpu.VMEM((2, LANE, HALF), BF),
        pltpu.VMEM((TOKENS, HALF), BF),
        pltpu.VMEM((2, CHIPS * LANE, TOKENS), BF),
        pltpu.VMEM((2, LANE, LANE), BF),
        pltpu.VMEM((TOKENS, LANE), F32),
        pltpu.VMEM((TOKENS, LANE), BF),
        pltpu.VMEM((TOKENS, LANE), F32),
        pltpu.VMEM((TOKENS, LANE), F32),
        pltpu.VMEM((TOKENS, LANE), F32),
        pltpu.VMEM((CHIPS, ROWS, ROWS), BF),
        pltpu.VMEM((CHIPS, ROWS, ROWS), BF),
        pltpu.VMEM((CHIPS, ROWS, ROWS), BF),
        pltpu.VMEM((CHIPS, ROWS, ROWS), BF),
        pltpu.VMEM((ROWS, HALF), F32),
        pltpu.VMEM((ROWS, HALF), BF),
        pltpu.VMEM((ROWS, HALF), F32),
        pltpu.VMEM((ROWS, HALF), BF),
        pltpu.VMEM((8, LANE), F32),
        pltpu.VMEM((8, LANE), F32),
        pltpu.VMEM((8, LANE), F32),
        pltpu.VMEM((8, LANE), F32),
        sem((5,)),
        sem((7,)),
        sem((7,)),
        sem((60,)),
        sem((CHIPS, 2, 2)),
        sem((60,)),
        sem((CHIPS, 2, 2)),
        sem((30,)),
        sem((CHIPS, 2, 1)),
        sem((CHIPS,)),
        sem((CHIPS,)),
        sem((CHIPS,)),
        sem((CHIPS,)),
        sem((2,)),
        sem,
        sem((2,)),
        sem,
    ]
    return pl.pallas_call(
        step_kernel,
        out_shape=(
            jax.ShapeDtypeStruct(stashed_inputs.shape, BF),
            jax.ShapeDtypeStruct(momentum.shape, BF),
            jax.ShapeDtypeStruct(momentum.shape, BF),
        ),
        in_specs=[anywhere] * 4,
        out_specs=(anywhere, anywhere, anywhere),
        scratch_shapes=scratch,
        compiler_params=pltpu.CompilerParams(
            collective_id=0, has_side_effects=True, vmem_limit_bytes=60 * 1024 * 1024),
        cost_estimate=pl.CostEstimate(
            flops=22 * 10**9, bytes_accessed=6 * 2**20, transcendentals=32768),
    )(cotangent, stashed_inputs, weights, momentum)


def solution(mesh):
    in_specs = (
        P(None, None, "dp"),
        P("pipe", None, None, "dp"),
        P("pipe", "dp", None),
        P("pipe", "dp", None),
    )
    out_specs = (P("pipe", None, None, "dp"), P("pipe", "dp", None), P("pipe", "dp", None))
    return jax.shard_map(
        per_device, mesh=mesh, in_specs=in_specs, out_specs=out_specs, check_vma=False
    )
```

```python
import functools
import math

import jax
import jax.numpy as jnp
from jax import lax
from jax.experimental import pallas as pl
from jax.experimental.pallas import tpu as pltpu
from jax.sharding import PartitionSpec as P

quintic_a = 3.4445
quintic_b = -4.775
quintic_c = 2.0315

MESH = pl.DeviceIdType.MESH
BF = jnp.bfloat16
F32 = jnp.float32
RING = 4
CHIPS = 16
LANE = 128
WIDTH = 4096
HALF = 2048
TOKENS = 256
ROWS = 256
OFFSETS = (0, 1, 3, 2)
NT = (((1,), (1,)), ((), ()))
NN = (((1,), (0,)), ((), ()))


def place():
    spot = lax.axis_index("dp")
    return lax.axis_index("pipe"), spot // 8, (spot // 2) % RING, spot % 2


def at(y, z, x, core):
    return (y, ((z % RING) * RING + x % RING) * 2 + core)


def chip_of(z, x):
    return (z % RING) * RING + x % RING


def multiple(value, of):
    return pl.multiple_of(value, of)


def ring(value, steps):
    return (value + steps) % RING


class Plane:
    def __init__(self):
        self.y, self.z, self.x, self.core = place()
        self.sibling = at(self.y, self.z, self.x, 1 - self.core)

    def own(self, part):
        return (self.x, self.z) if part == 0 else (self.z, self.x)

    def spot(self, part, first, second):
        own_first, own_second = self.own(part)
        return ring(own_first, first), ring(own_second, second)

    def target(self, part, axis, steps):
        along_x = (axis == 0) == (part == 0)
        if along_x:
            return at(self.y, self.z, self.x + steps, self.core)
        return at(self.y, self.z + steps, self.x, self.core)

    def remote(self, src, dst, send_sem, recv_sem, device=None):
        return pltpu.make_async_remote_copy(
            src_ref=src, dst_ref=dst, send_sem=send_sem, recv_sem=recv_sem,
            device_id=self.sibling if device is None else device, device_id_type=MESH,
        )


class TwoStage:
    def __init__(self, plane, slot, send, recv):
        self.plane, self.slot, self.send, self.recv = plane, slot, send, recv

    def copy(self, part, first, second, axis, steps, number):
        one, two = self.plane.spot(part, first, second)
        z, x = (two, one) if part == 0 else (one, two)
        ref = self.slot(z, x, part)
        return self.plane.remote(ref, ref, self.send.at[number], self.recv.at[part, one * RING + two],
                                 self.plane.target(part, axis, steps))

    def wait(self, part, first, second):
        self.copy(part, first, second, 0, 1, 0).wait_recv()

    def start(self):
        number = 0
        for axis in (0, 1):
            for steps in (1, 3, 2):
                for part in (0, 1):
                    self.copy(part, 0, 0, axis, steps, number).start()
                    number += 1

    def forward(self):
        number = 12
        for first in (1, 3, 2):
            for part in (0, 1):
                self.wait(part, first, 0)
                for steps in (1, 3, 2):
                    self.copy(part, first, 0, 1, steps, number).start()
                    number += 1

    def finish(self):
        for first in (0, 1, 3, 2):
            for part in (0, 1):
                for second in (1, 3, 2):
                    self.wait(part, first, second)

    def drain(self):
        def body(number, carry):
            self.copy(0, 0, 0, 0, 1, number).wait_send()
            return carry

        lax.fori_loop(0, 30, body, 0)


DEPTH = 2
CHUNKS = ((0, 1, 2), (3, 4), (5, 6, 7))


class Bulk:
    def __init__(self, plane, buf, send, recv):
        self.plane, self.buf, self.send, self.recv = plane, buf, send, recv

    def copy(self, part, first, second, half, axis, steps, number):
        one, two = self.plane.spot(part, first, second)
        row = part * HALF + (one * RING + two) * LANE + half * 64
        ref = self.buf.at[pl.ds(multiple(row, 64), 64), :]
        return self.plane.remote(ref, ref, self.send.at[number], self.recv.at[part, one * RING + two, half],
                                 self.plane.target(part, axis, steps))

    def wait(self, first, second, half):
        for part in (0, 1):
            self.copy(part, first, second, half, 0, 1, 0).wait_recv()

    def sent(self, number):
        for k in range(4):
            self.copy(0, 0, 0, 0, 0, 1, number * 4 + k).wait_send()

    def put(self, number, plus, minus, axis):
        if number >= DEPTH:
            self.sent(number - DEPTH)
        for k, (what, steps) in enumerate(((plus, 1), (minus, 3))):
            for part in (0, 1):
                self.copy(part, *what, axis, steps, number * 4 + k * 2 + part).start()

    def spread(self, number, first, half):
        self.put(number, (first, 0, half), (first, 0, half), 1)

    def pass_on(self, number, first):
        self.wait(first, 3, 0)
        self.wait(first, 1, 1)
        self.put(number, (first, 3, 0), (first, 1, 1), 1)

    def round(self, number):
        if number < 2:
            self.put(number, (0, 0, number), (0, 0, number), 0)
        elif number < 4:
            self.spread(number, 0, number - 2)
        elif number == 4:
            self.wait(3, 0, 0)
            self.wait(1, 0, 1)
            self.put(number, (3, 0, 0), (1, 0, 1), 0)
        elif number == 5:
            self.wait(1, 0, 0)
            self.spread(number, 1, 0)
        elif number == 6:
            self.spread(number, 1, 1)
        elif number == 7:
            self.pass_on(number, 0)
        elif number == 8:
            self.spread(number, 3, 0)
        elif number == 9:
            self.wait(3, 0, 1)
            self.spread(number, 3, 1)
        elif number == 10:
            self.pass_on(number, 1)
        elif number in (11, 12):
            self.wait(2, 0, number - 11)
            self.spread(number, 2, number - 11)
        elif number == 13:
            self.pass_on(number, 3)
        elif number == 14:
            self.pass_on(number, 2)

    def complete(self, first):
        self.wait(first, 1, 0)
        self.wait(first, 3, 1)
        self.wait(first, 2, 0)
        self.wait(first, 2, 1)


def step_kernel(
    cot, xs, w, m, dout, nout, oout,
    mbuf, nbuf, nrow, wbuf, ubuf, gbuf, xin, slope, dbuf, bsend, brecv, bown, apart, aother, fpart, fother,
    eacc, ebf, qacc, obuf, own_sum, other_sum, sum_x, sum_z,
    lsem, sib_send, sib_recv, msend, mrecv, gsend, grecv, usend, urecv,
    asend, arecv, fsend, frecv, osem, orecv, nsem, nrecv, ssend, srecv,
):
    plane = Plane()
    y, z, x, core = plane.y, plane.z, plane.x, plane.core
    remote = plane.remote
    me = chip_of(z, x)
    own_spot = (1 - core) * (x * RING + z) + core * (z * RING + x)

    partners = [at(y, z, x + 1, core), at(y, z, x + 2, core), at(y, z, x + 3, core),
                at(y, z + 1, x, core), at(y, z + 2, x, core), at(y, z + 3, x, core),
                plane.sibling, at(ring(y, 1), z, x, core), at(ring(y, 3), z, x, core)]
    load_x = pltpu.make_async_copy(xs.at[0], xin, lsem.at[0])
    load_x.start()
    barrier = pltpu.get_barrier_semaphore()
    for partner in partners:
        pl.semaphore_signal(barrier, 1, device_id=partner, device_id_type=MESH)

    own_m = mbuf.at[pl.ds(multiple(core * HALF + own_spot * LANE, LANE), LANE), :]

    def own_columns(k, core_at):
        return pl.ds(multiple((2 * k + core_at) * LANE, LANE), LANE)

    def load_own(k, carry):
        lanes = pl.ds(multiple(k * LANE, LANE), LANE)
        pltpu.make_async_copy(m.at[0, :, own_columns(k, core)], own_m.at[:, lanes], lsem.at[1]).start()
        pltpu.make_async_copy(w.at[0, :, own_columns(k, core)], wbuf.at[core, :, lanes], lsem.at[2]).start()
        return carry

    lax.fori_loop(0, CHIPS, load_own, 0)
    pl.semaphore_wait(barrier, len(partners))

    def give_sibling(k, carry):
        lanes = pl.ds(multiple(k * LANE, LANE), LANE)
        remote(m.at[0, :, own_columns(k, 1 - core)], own_m.at[:, lanes], sib_send.at[0], sib_recv.at[0]).start()
        remote(w.at[0, :, own_columns(k, 1 - core)], wbuf.at[core, :, lanes],
               sib_send.at[1], sib_recv.at[1]).start()
        return carry

    lax.fori_loop(0, CHIPS, give_sibling, 0)

    load_x.wait()
    values = xin[...].reshape(TOKENS, LANE).astype(F32)
    sigmoid_val = jax.nn.sigmoid(values)
    slope[...] = sigmoid_val * (1.0 + values * (1.0 - sigmoid_val))
    gated = (values * sigmoid_val).astype(BF).astype(F32)
    gbuf[core, pl.ds(multiple(own_spot * LANE, LANE), LANE), :] = jnp.transpose(gated).astype(BF)

    def g_slot(z_at, x_at, part):
        spot = (1 - core) * (x_at * RING + z_at) + core * (z_at * RING + x_at)
        return gbuf.at[core, pl.ds(multiple(spot * LANE + part * 64, 64), 64), :]

    def u_slot(z_at, x_at, part):
        return ubuf.at[pl.ds(part * LANE, LANE), pl.ds(multiple((z_at * RING + x_at) * LANE, LANE), LANE)]

    bulk = Bulk(plane, mbuf, msend, mrecv)
    gather_g = TwoStage(plane, g_slot, gsend, grecv)
    gather_u = TwoStage(plane, u_slot, usend, urecv)
    gather_g.start()

    own_u = ubuf.at[:, pl.ds(multiple(me * LANE, LANE), LANE)]

    def from_above():
        return remote(dbuf, own_u, sib_send.at[3], sib_recv.at[3], at(ring(y, 3), z, x, core))

    def chain():
        @pl.when(y == RING - 1)
        def _():
            for micro in range(2):
                pltpu.make_async_copy(
                    cot.at[micro],
                    ubuf.at[pl.ds(micro * LANE, LANE), pl.ds(multiple(me * LANE, LANE), LANE)],
                    lsem.at[3]).start()
            pltpu.make_async_copy(own_u, own_u, lsem.at[3]).wait()

        @pl.when(y < RING - 1)
        def _():
            from_above().wait_recv()

        gather_u.start()
        gather_u.forward()
        pltpu.make_async_copy(wbuf.at[core], wbuf.at[core], lsem.at[2]).wait()
        remote(wbuf.at[core], wbuf.at[core], sib_send.at[1], sib_recv.at[1]).wait_recv()
        gather_u.finish()
        full = ubuf[...]
        bsend[...] = lax.dot_general(full, wbuf[1 - core], NT, preferred_element_type=F32)
        give = remote(bsend, brecv, sib_send.at[2], sib_recv.at[2])
        give.start()
        bown[...] = lax.dot_general(full, wbuf[core], NT, preferred_element_type=F32)
        give.wait()
        back = bown[...] + brecv[...]
        upstream = ubuf[:, pl.ds(multiple(me * LANE, LANE), LANE)].astype(F32)
        dbuf[...] = (upstream + slope[...] * back).astype(BF)

        @pl.when(y > 0)
        def _():
            from_above().start()

        for micro in range(2):
            pltpu.make_async_copy(
                dbuf.at[pl.ds(micro * LANE, LANE), :], dout.at[0, micro], lsem.at[4]).start()

    pltpu.make_async_copy(own_m, own_m, lsem.at[1]).wait()
    remote(own_m, own_m, sib_send.at[0], sib_recv.at[0]).wait_recv()

    def front(index, carry):
        @pl.when(index == RING - 1 - y)
        def _():
            chain()

        for which, rounds in enumerate(CHUNKS):
            @pl.when(index == which)
            def _(which=which, rounds=rounds):
                if which == 1:
                    gather_g.forward()
                for number in rounds:
                    bulk.round(number)
        return carry

    lax.fori_loop(0, RING, front, 0)

    def share(part):
        return remote(gbuf.at[part], gbuf.at[part], sib_send.at[4], sib_recv.at[4])

    gather_g.finish()
    share(core).start()

    share(1 - core).wait_recv()
    sums = jnp.zeros((8, LANE), F32)
    for part in (0, 1):
        one, two = plane.own(part)
        spot = one * RING + two
        grad = lax.dot_general(
            gbuf[part, pl.ds(multiple(spot * LANE, LANE), LANE), :], ubuf[...], NN,
            preferred_element_type=F32)
        old = mbuf[pl.ds(multiple(part * HALF + spot * LANE, LANE), LANE), :].astype(F32)
        fresh = (0.95 * old + grad).astype(BF)
        nrow[pl.ds(part * LANE, LANE), :] = fresh
        wide = fresh.astype(F32)
        square = wide * wide
        for k in range(CHIPS):
            sums = sums + jnp.sum(
                square[:, k * LANE:(k + 1) * LANE].reshape(16, 8, LANE), axis=0)
    own_sum[...] = sums
    swap = remote(own_sum, other_sum, sib_send.at[5], sib_recv.at[5])
    swap.start()

    def give_rows(buf, out, sem, recv):
        def body(k, carry):
            lanes = pl.ds(multiple(k * LANE, LANE), LANE)
            pltpu.make_async_copy(
                buf.at[pl.ds(multiple(core * LANE, LANE), LANE), lanes],
                out.at[0, :, own_columns(k, core)], sem.at[0]).start()
            remote(buf.at[pl.ds(multiple((1 - core) * LANE, LANE), LANE), lanes],
                   out.at[0, :, own_columns(k, core)], sem.at[1], recv).start()
            return carry

        lax.fori_loop(0, CHIPS, body, 0)

    def wait_rows(buf, sem, recv):
        half = buf.at[pl.ds(0, LANE), :]
        pltpu.make_async_copy(half, half, sem.at[0]).wait()
        both = remote(half, half, sem.at[1], recv)
        both.wait_send()
        both.wait_recv()

    give_rows(nrow, nout, nsem, nrecv)

    def to_ring(buf, axis, steps, own):
        return remote(buf.at[own], buf.at[own], ssend.at[axis, steps - 1], srecv.at[axis, own],
                      plane.target(0, axis, steps))

    def start_ring(buf, axis, own, value):
        buf[own] = value
        for steps in (1, 2, 3):
            to_ring(buf, axis, steps, own).start()

    def wait_ring(buf, axis, own):
        for steps in (1, 2, 3):
            to_ring(buf, axis, steps, ring(own, steps)).wait_recv()
        return buf[0] + buf[1] + buf[2] + buf[3]

    def group_rows(index, part):
        first = plane.spot(part, OFFSETS[index], 0)[0]
        return part, multiple(first * 512, 512)

    def a_copy(slot):
        return remote(apart.at[slot], aother.at[slot], asend.at[slot], arecv.at[slot])

    def f_copy(slot):
        return remote(fpart.at[slot], fother.at[slot], fsend.at[slot], frecv.at[slot])

    def build(index):
        for part in (0, 1):
            part, start = group_rows(index, part)
            rows = pl.ds(part * HALF + start, 512)
            grad = lax.dot_general(gbuf[part, pl.ds(start, 512), :], ubuf[...], NN,
                                   preferred_element_type=F32)
            nbuf[rows, :] = (0.95 * mbuf[rows, :].astype(F32) + grad).astype(BF)

    def gram(index):
        for part in (0, 1):
            part, start = group_rows(index, part)
            rows = pl.ds(part * HALF + start, 512)
            product = lax.dot_general(nrow[...], nbuf[rows, :], NT, preferred_element_type=F32)
            apart[index * 2 + part] = (product * inverse).astype(BF)
            a_copy(index * 2 + part).start()

    def cubic(index):
        for part in (0, 1):
            part, start = group_rows(index, part)
            rows = pl.ds(part * HALF + start, 512)
            slot = index * 2 + part
            a_copy(slot).wait_recv()
            whole = (apart[slot].astype(F32) + aother[slot].astype(F32)).astype(BF)
            product = lax.dot_general(whole, nbuf[rows, :], NN, preferred_element_type=F32)
            if slot == 0:
                eacc[...] = product
            else:
                eacc[...] += product

    bulk.round(8)
    swap.wait()
    chip_sum = own_sum[...] + other_sum[...]
    start_ring(sum_x, 0, x, chip_sum)
    chip_norm = jnp.sqrt(jnp.maximum(jnp.sum(chip_sum), 1e-30))
    inverse = 1.0 / chip_norm
    bulk.complete(OFFSETS[0])
    build(0)
    bulk.round(9)
    gram(0)
    bulk.round(10)
    cubic(0)
    bulk.round(11)
    start_ring(sum_z, 1, z, wait_ring(sum_x, 0, x))
    bulk.complete(OFFSETS[1])
    build(1)
    bulk.round(12)
    gram(1)
    bulk.round(13)
    cubic(1)
    bulk.complete(OFFSETS[2])
    build(2)
    bulk.round(14)
    gram(2)
    cubic(2)
    sum_squares = jnp.sum(wait_ring(sum_z, 1, z))
    scaling = 0.4 / jnp.sqrt(float(WIDTH) * (sum_squares / float(WIDTH * WIDTH) + 1e-06))
    bulk.complete(OFFSETS[3])
    build(3)
    gram(3)
    cubic(3)
    ebf[...] = (((eacc[...] * scaling) * scaling) * (scaling * chip_norm)).astype(BF)

    def back_part(slot):
        product = lax.dot_general(ebf[...], nbuf[pl.ds(slot * 1024, 1024), :], NT, preferred_element_type=F32)
        fpart[slot] = (product * scaling).astype(BF)
        f_copy(slot).start()

    def quintic(slot):
        f_copy(slot).wait_recv()
        whole = (fpart[slot].astype(F32) + fother[slot].astype(F32)).astype(BF)
        product = lax.dot_general(whole, nbuf[pl.ds(slot * 1024, 1024), :], NN, preferred_element_type=F32)
        if slot == 0:
            qacc[...] = product
        else:
            qacc[...] += product

    for slot in range(4):
        back_part(slot)
    for slot in range(4):
        quintic(slot)
    scaled = (nrow[...].astype(F32) * scaling).astype(BF).astype(F32)
    mixed = (quintic_a * scaled + quintic_b * ebf[...].astype(F32)
             + quintic_c * (qacc[...] * scaling))
    obuf[...] = (math.sqrt(WIDTH) * mixed).astype(BF)
    give_rows(obuf, oout, osem, orecv)

    @pl.when(y > 0)
    def _():
        from_above().wait_send()

    pltpu.make_async_copy(dbuf, dbuf, lsem.at[4]).wait()
    remote(own_m, own_m, sib_send.at[0], sib_recv.at[0]).wait_send()
    remote(wbuf.at[core], wbuf.at[core], sib_send.at[1], sib_recv.at[1]).wait_send()
    share(core).wait_send()
    for number in range(15 - DEPTH, 15):
        bulk.sent(number)
    gather_g.drain()
    gather_u.drain()
    for axis, buf in enumerate((sum_x, sum_z)):
        for steps in (1, 2, 3):
            to_ring(buf, axis, steps, 0).wait_send()
    for slot in range(8):
        a_copy(slot).wait_send()
    for slot in range(4):
        f_copy(slot).wait_send()
    wait_rows(nrow, nsem, nrecv)
    wait_rows(obuf, osem, orecv)


def per_device(cotangent, stashed_inputs, weights, momentum):
    anywhere = pl.BlockSpec(memory_space=pl.ANY)
    sem = pltpu.SemaphoreType.DMA
    scratch = [
        pltpu.VMEM((WIDTH, HALF), BF),
        pltpu.VMEM((WIDTH, HALF), BF),
        pltpu.VMEM((ROWS, HALF), BF),
        pltpu.VMEM((2, LANE, HALF), BF),
        pltpu.VMEM((TOKENS, HALF), BF),
        pltpu.VMEM((2, HALF, TOKENS), BF),
        pltpu.VMEM((2, LANE, LANE), BF),
        pltpu.VMEM((TOKENS, LANE), F32),
        pltpu.VMEM((TOKENS, LANE), BF),
        pltpu.VMEM((TOKENS, LANE), F32),
        pltpu.VMEM((TOKENS, LANE), F32),
        pltpu.VMEM((TOKENS, LANE), F32),
        pltpu.VMEM((8, ROWS, 512), BF),
        pltpu.VMEM((8, ROWS, 512), BF),
        pltpu.VMEM((4, ROWS, 1024), BF),
        pltpu.VMEM((4, ROWS, 1024), BF),
        pltpu.VMEM((ROWS, HALF), F32),
        pltpu.VMEM((ROWS, HALF), BF),
        pltpu.VMEM((ROWS, HALF), F32),
        pltpu.VMEM((ROWS, HALF), BF),
        pltpu.VMEM((8, LANE), F32),
        pltpu.VMEM((8, LANE), F32),
        pltpu.VMEM((RING, 8, LANE), F32),
        pltpu.VMEM((RING, 8, LANE), F32),
        sem((5,)),
        sem((6,)),
        sem((6,)),
        sem((60,)),
        sem((2, CHIPS, 2)),
        sem((30,)),
        sem((2, CHIPS)),
        sem((30,)),
        sem((2, CHIPS)),
        sem((8,)),
        sem((8,)),
        sem((4,)),
        sem((4,)),
        sem((2,)),
        sem,
        sem((2,)),
        sem,
        sem((2, 3)),
        sem((2, RING)),
    ]
    return pl.pallas_call(
        step_kernel,
        out_shape=(
            jax.ShapeDtypeStruct(stashed_inputs.shape, BF),
            jax.ShapeDtypeStruct(momentum.shape, BF),
            jax.ShapeDtypeStruct(momentum.shape, BF),
        ),
        in_specs=[anywhere] * 4,
        out_specs=(anywhere, anywhere, anywhere),
        scratch_shapes=scratch,
        compiler_params=pltpu.CompilerParams(
            collective_id=0, has_side_effects=True, vmem_limit_bytes=60 * 1024 * 1024),
        cost_estimate=pl.CostEstimate(
            flops=22 * 10**9, bytes_accessed=6 * 2**20, transcendentals=32768),
    )(cotangent, stashed_inputs, weights, momentum)


def solution(mesh):
    in_specs = (
        P(None, None, "dp"),
        P("pipe", None, None, "dp"),
        P("pipe", "dp", None),
        P("pipe", "dp", None),
    )
    out_specs = (P("pipe", None, None, "dp"), P("pipe", "dp", None), P("pipe", "dp", None))
    return jax.shard_map(
        per_device, mesh=mesh, in_specs=in_specs, out_specs=out_specs, check_vma=False
    )
```

```python
import functools
import math

import jax
import jax.numpy as jnp
from jax import lax
from jax.experimental import pallas as pl
from jax.experimental.pallas import tpu as pltpu
from jax.sharding import PartitionSpec as P

quintic_a = 3.4445
quintic_b = -4.775
quintic_c = 2.0315

MESH = pl.DeviceIdType.MESH
BF = jnp.bfloat16
F32 = jnp.float32
RING = 4
CHIPS = 16
LANE = 128
WIDTH = 4096
HALF = 2048
TOKENS = 256
ROWS = 256
OFFSETS = (0, 1, 3, 2)
NT = (((1,), (1,)), ((), ()))
NN = (((1,), (0,)), ((), ()))


def place():
    spot = lax.axis_index("dp")
    return lax.axis_index("pipe"), spot // 8, (spot // 2) % RING, spot % 2


def at(y, z, x, core):
    return (y, ((z % RING) * RING + x % RING) * 2 + core)


def chip_of(z, x):
    return (z % RING) * RING + x % RING


def multiple(value, of):
    return pl.multiple_of(value, of)


def ring(value, steps):
    return (value + steps) % RING


class Plane:
    def __init__(self):
        self.y, self.z, self.x, self.core = place()
        self.sibling = at(self.y, self.z, self.x, 1 - self.core)

    def own(self, part):
        return (self.x, self.z) if part == 0 else (self.z, self.x)

    def spot(self, part, first, second):
        own_first, own_second = self.own(part)
        return ring(own_first, first), ring(own_second, second)

    def target(self, part, axis, steps):
        along_x = (axis == 0) == (part == 0)
        if along_x:
            return at(self.y, self.z, self.x + steps, self.core)
        return at(self.y, self.z + steps, self.x, self.core)

    def remote(self, src, dst, send_sem, recv_sem, device=None):
        return pltpu.make_async_remote_copy(
            src_ref=src, dst_ref=dst, send_sem=send_sem, recv_sem=recv_sem,
            device_id=self.sibling if device is None else device, device_id_type=MESH,
        )


class TwoStage:
    def __init__(self, plane, slot, send, recv):
        self.plane, self.slot, self.send, self.recv = plane, slot, send, recv

    def copy(self, part, first, second, axis, steps, number):
        one, two = self.plane.spot(part, first, second)
        z, x = (two, one) if part == 0 else (one, two)
        ref = self.slot(z, x, part)
        return self.plane.remote(ref, ref, self.send.at[number], self.recv.at[part, one * RING + two],
                                 self.plane.target(part, axis, steps))

    def wait(self, part, first, second):
        self.copy(part, first, second, 0, 1, 0).wait_recv()

    def start(self):
        number = 0
        for axis in (0, 1):
            for steps in (1, 3, 2):
                for part in (0, 1):
                    self.copy(part, 0, 0, axis, steps, number).start()
                    number += 1

    def forward(self):
        number = 12
        for first in (1, 3, 2):
            for part in (0, 1):
                self.wait(part, first, 0)
                for steps in (1, 3, 2):
                    self.copy(part, first, 0, 1, steps, number).start()
                    number += 1

    def finish(self):
        for first in (0, 1, 3, 2):
            for part in (0, 1):
                for second in (1, 3, 2):
                    self.wait(part, first, second)

    def drain(self):
        def body(number, carry):
            self.copy(0, 0, 0, 0, 1, number).wait_send()
            return carry

        lax.fori_loop(0, 30, body, 0)


DEPTH = 2
CHUNKS = ((0, 1), (2, 3, 4), (5, 6))
EXTRA = {3: (0, 1), 2: (2, 3), 1: (5,), 0: (7, 8)}


class Bulk:
    def __init__(self, plane, buf, send, recv):
        self.plane, self.buf, self.send, self.recv = plane, buf, send, recv

    def copy(self, part, first, second, half, axis, steps, number):
        one, two = self.plane.spot(part, first, second)
        row = part * HALF + (one * RING + two) * LANE + half * 64
        ref = self.buf.at[pl.ds(multiple(row, 64), 64), :]
        return self.plane.remote(ref, ref, self.send.at[number], self.recv.at[part, one * RING + two, half],
                                 self.plane.target(part, axis, steps))

    def wait(self, first, second, half):
        for part in (0, 1):
            self.copy(part, first, second, half, 0, 1, 0).wait_recv()

    def sent(self, number):
        for k in range(4):
            self.copy(0, 0, 0, 0, 0, 1, number * 4 + k).wait_send()

    def put(self, number, plus, minus, axis):
        if number >= DEPTH:
            self.sent(number - DEPTH)
        for k, (what, steps) in enumerate(((plus, 1), (minus, 3))):
            for part in (0, 1):
                self.copy(part, *what, axis, steps, number * 4 + k * 2 + part).start()

    def spread(self, number, first, half):
        self.put(number, (first, 0, half), (first, 0, half), 1)

    def pass_on(self, number, first):
        self.wait(first, 3, 0)
        self.wait(first, 1, 1)
        self.put(number, (first, 3, 0), (first, 1, 1), 1)

    def round(self, number):
        if number < 2:
            self.put(number, (0, 0, number), (0, 0, number), 0)
        elif number < 4:
            self.spread(number, 0, number - 2)
        elif number == 4:
            self.wait(3, 0, 0)
            self.wait(1, 0, 1)
            self.put(number, (3, 0, 0), (1, 0, 1), 0)
        elif number == 5:
            self.wait(1, 0, 0)
            self.spread(number, 1, 0)
        elif number == 6:
            self.spread(number, 1, 1)
        elif number == 7:
            self.pass_on(number, 0)
        elif number == 8:
            self.spread(number, 3, 0)
        elif number == 9:
            self.wait(3, 0, 1)
            self.spread(number, 3, 1)
        elif number == 10:
            self.pass_on(number, 1)
        elif number in (11, 12):
            self.wait(2, 0, number - 11)
            self.spread(number, 2, number - 11)
        elif number == 13:
            self.pass_on(number, 3)
        elif number == 14:
            self.pass_on(number, 2)

    def complete(self, first):
        self.wait(first, 1, 0)
        self.wait(first, 3, 1)
        self.wait(first, 2, 0)
        self.wait(first, 2, 1)


def step_kernel(
    cot, xs, w, m, dout, nout, oout,
    mbuf, nbuf, nrow, wbuf, ubuf, gbuf, xin, slope, dbuf, bsend, brecv, bown, apart, aother, fpart, fother,
    eacc, ebf, fwhole, stage, own_sum, other_sum, sum_x, sum_z,
    lsem, sib_send, sib_recv, msend, mrecv, gsend, grecv, usend, urecv,
    asend, arecv, fsend, frecv, osem, orecv, nsem, nrecv, ssend, srecv,
):
    plane = Plane()
    y, z, x, core = plane.y, plane.z, plane.x, plane.core
    remote = plane.remote
    me = chip_of(z, x)
    own_spot = (1 - core) * (x * RING + z) + core * (z * RING + x)

    partners = [at(y, z, x + 1, core), at(y, z, x + 2, core), at(y, z, x + 3, core),
                at(y, z + 1, x, core), at(y, z + 2, x, core), at(y, z + 3, x, core),
                plane.sibling, at(ring(y, 1), z, x, core), at(ring(y, 3), z, x, core)]
    load_x = pltpu.make_async_copy(xs.at[0], xin, lsem.at[0])
    own_u = ubuf.at[:, pl.ds(multiple(me * LANE, LANE), LANE)]
    barrier = pltpu.get_barrier_semaphore()
    for partner in partners:
        pl.semaphore_signal(barrier, 1, device_id=partner, device_id_type=MESH)

    @pl.when(y == RING - 1)
    def _():
        for micro in range(2):
            pltpu.make_async_copy(
                cot.at[micro],
                ubuf.at[pl.ds(micro * LANE, LANE), pl.ds(multiple(me * LANE, LANE), LANE)],
                lsem.at[3]).start()

    load_x.start()
    own_m = mbuf.at[pl.ds(multiple(core * HALF + own_spot * LANE, LANE), LANE), :]

    def load_rows(src, at_stage, which):
        for half in (0, 1):
            pltpu.make_async_copy(src.at[0, :, pl.ds(half * HALF, HALF)],
                                  stage.at[at_stage, pl.ds(half * LANE, LANE), :], lsem.at[which]).start()

    def given(at_stage, dst, which):
        return remote(stage.at[at_stage + 1, pl.ds(0, LANE), :], dst, sib_send.at[which], sib_recv.at[which])

    def split_rows(at_stage, dst, which, own_which):
        whole = stage.at[at_stage]
        pltpu.make_async_copy(whole, whole, lsem.at[own_which]).wait()
        for k in range(CHIPS):
            half, lanes = k // 8, pl.ds(k * LANE, LANE)
            for mine in (1, 0):
                which_core = core if mine else 1 - core
                source = pl.ds(multiple((2 * (k % 8) + which_core) * LANE, LANE), LANE)
                piece = stage[at_stage, pl.ds(half * LANE, LANE), source]
                if mine:
                    dst[:, lanes] = piece
                else:
                    stage[at_stage + 1, pl.ds(0, LANE), lanes] = piece
        given(at_stage, dst, which).start()

    load_rows(m, 0, 1)
    load_rows(w, 2, 2)
    pl.semaphore_wait(barrier, len(partners))

    def u_slot(z_at, x_at, part):
        return ubuf.at[pl.ds(part * LANE, LANE), pl.ds(multiple((z_at * RING + x_at) * LANE, LANE), LANE)]

    gather_u = TwoStage(plane, u_slot, usend, urecv)

    @pl.when(y == RING - 1)
    def _():
        pltpu.make_async_copy(own_u, own_u, lsem.at[3]).wait()
        gather_u.start()

    split_rows(0, own_m, 0, 1)

    load_x.wait()
    values = xin[...].reshape(TOKENS, LANE).astype(F32)
    sigmoid_val = jax.nn.sigmoid(values)
    slope[...] = sigmoid_val * (1.0 + values * (1.0 - sigmoid_val))
    gated = (values * sigmoid_val).astype(BF).astype(F32)
    gbuf[core, pl.ds(multiple(own_spot * LANE, LANE), LANE), :] = jnp.transpose(gated).astype(BF)

    def load_weights():
        split_rows(2, wbuf.at[core], 1, 2)

    def g_slot(z_at, x_at, part):
        spot = (1 - core) * (x_at * RING + z_at) + core * (z_at * RING + x_at)
        return gbuf.at[core, pl.ds(multiple(spot * LANE + part * 64, 64), 64), :]

    bulk = Bulk(plane, mbuf, msend, mrecv)
    gather_g = TwoStage(plane, g_slot, gsend, grecv)

    def from_above():
        return remote(dbuf, own_u, sib_send.at[3], sib_recv.at[3], at(ring(y, 3), z, x, core))

    def own_rows_here():
        given(0, own_m, 0).wait()

    def go(number):
        taken = [at_y for at_y, rounds in EXTRA.items() if number in rounds]
        if not taken:
            bulk.round(number)
        else:
            @pl.when(y != taken[0])
            def _():
                bulk.round(number)

    def chain():
        @pl.when(y < RING - 1)
        def _():
            from_above().wait_recv()
            gather_u.start()

        gather_u.forward()
        for at_y, rounds in EXTRA.items():
            @pl.when(y == at_y)
            def _(rounds=rounds, at_y=at_y):
                if at_y == RING - 1:
                    gather_g.start()
                    own_rows_here()
                    load_weights()
                for number in rounds:
                    bulk.round(number)

        gather_u.finish()

        @pl.when(y > 0)
        def _():
            back_product()

    def back_product():
        given(2, wbuf.at[core], 1).wait()
        full = ubuf[...]
        bsend[...] = lax.dot_general(full, wbuf[1 - core], NT, preferred_element_type=F32)
        give = remote(bsend, brecv, sib_send.at[2], sib_recv.at[2])
        give.start()
        bown[...] = lax.dot_general(full, wbuf[core], NT, preferred_element_type=F32)
        give.wait()
        back = bown[...] + brecv[...]
        upstream = ubuf[:, pl.ds(multiple(me * LANE, LANE), LANE)].astype(F32)
        dbuf[...] = (upstream + slope[...] * back).astype(BF)

        @pl.when(y > 0)
        def _():
            from_above().start()

        for micro in range(2):
            pltpu.make_async_copy(
                dbuf.at[pl.ds(micro * LANE, LANE), :], dout.at[0, micro], lsem.at[4]).start()

    def front(index, carry):
        @pl.when(index == RING - 1 - y)
        def _():
            chain()

        for which, rounds in enumerate(CHUNKS):
            @pl.when(index == which)
            def _(which=which, rounds=rounds):
                if which == 0:
                    @pl.when(y < RING - 1)
                    def _():
                        gather_g.start()
                        own_rows_here()
                        load_weights()
                if which == 1:
                    gather_g.forward()
                for number in rounds:
                    go(number)
        return carry

    lax.fori_loop(0, RING, front, 0)

    go(7)

    def share(part):
        return remote(gbuf.at[part], gbuf.at[part], sib_send.at[4], sib_recv.at[4])

    gather_g.finish()
    share(core).start()

    share(1 - core).wait_recv()
    sums = jnp.zeros((8, LANE), F32)
    for part in (0, 1):
        one, two = plane.own(part)
        spot = one * RING + two
        grad = lax.dot_general(
            gbuf[part, pl.ds(multiple(spot * LANE, LANE), LANE), :], ubuf[...], NN,
            preferred_element_type=F32)
        old = mbuf[pl.ds(multiple(part * HALF + spot * LANE, LANE), LANE), :].astype(F32)
        fresh = (0.95 * old + grad).astype(BF)
        nrow[pl.ds(part * LANE, LANE), :] = fresh
        wide = fresh.astype(F32)
        square = wide * wide
        for k in range(CHIPS):
            sums = sums + jnp.sum(
                square[:, k * LANE:(k + 1) * LANE].reshape(16, 8, LANE), axis=0)
    own_sum[...] = sums
    swap = remote(own_sum, other_sum, sib_send.at[5], sib_recv.at[5])
    swap.start()

    def give_rows(buf, out, sem, recv, lanes=pl.ds(0, HALF)):
        pltpu.make_async_copy(
            buf.at[pl.ds(multiple(core * LANE, LANE), LANE), lanes], out.at[core, :, lanes], sem.at[0]).start()
        remote(buf.at[pl.ds(multiple((1 - core) * LANE, LANE), LANE), lanes], out.at[core, :, lanes],
               sem.at[1], recv).start()

    def wait_rows(buf, sem, recv):
        half = buf.at[pl.ds(0, LANE), :]
        pltpu.make_async_copy(half, half, sem.at[0]).wait()
        both = remote(half, half, sem.at[1], recv)
        both.wait_send()
        both.wait_recv()

    give_rows(nrow, nout, nsem, nrecv)

    def to_ring(buf, axis, steps, own):
        return remote(buf.at[own], buf.at[own], ssend.at[axis, steps - 1], srecv.at[axis, own],
                      plane.target(0, axis, steps))

    def start_ring(buf, axis, own, value):
        buf[own] = value
        for steps in (1, 2, 3):
            to_ring(buf, axis, steps, own).start()

    def wait_ring(buf, axis, own):
        for steps in (1, 2, 3):
            to_ring(buf, axis, steps, ring(own, steps)).wait_recv()
        return buf[0] + buf[1] + buf[2] + buf[3]

    def group_rows(index, part):
        first = plane.spot(part, OFFSETS[index], 0)[0]
        return part, multiple(first * 512, 512)

    def a_copy(slot):
        return remote(apart.at[slot], aother.at[slot], asend.at[slot], arecv.at[slot])

    def f_copy(slot):
        return remote(fpart.at[slot], fother.at[slot], fsend.at[slot], frecv.at[slot])

    def build(index):
        for part in (0, 1):
            part, start = group_rows(index, part)
            rows = pl.ds(part * HALF + start, 512)
            grad = lax.dot_general(gbuf[part, pl.ds(start, 512), :], ubuf[...], NN,
                                   preferred_element_type=F32)
            nbuf[rows, :] = (0.95 * mbuf[rows, :].astype(F32) + grad).astype(BF)

    def gram(index):
        for part in (0, 1):
            part, start = group_rows(index, part)
            rows = pl.ds(part * HALF + start, 512)
            product = lax.dot_general(nrow[...], nbuf[rows, :], NT, preferred_element_type=F32)
            apart[index * 2 + part] = (product * inverse).astype(BF)
            a_copy(index * 2 + part).start()

    def cubic(index):
        for part in (0, 1):
            part, start = group_rows(index, part)
            rows = pl.ds(part * HALF + start, 512)
            slot = index * 2 + part
            a_copy(slot).wait_recv()
            whole = (apart[slot].astype(F32) + aother[slot].astype(F32)).astype(BF)
            product = lax.dot_general(whole, nbuf[rows, :], NN, preferred_element_type=F32)
            if slot == 0:
                eacc[...] = product
            else:
                eacc[...] += product

    def small(second):
        parts = []
        for part in (0, 1):
            first, last = plane.spot(part, OFFSETS[3], second)
            start = multiple((first * RING + last) * LANE, LANE)
            rows = pl.ds(part * HALF + start, LANE)
            grad = lax.dot_general(gbuf[part, pl.ds(start, LANE), :], ubuf[...], NN,
                                   preferred_element_type=F32)
            fresh = (0.95 * mbuf[rows, :].astype(F32) + grad).astype(BF)
            nbuf[rows, :] = fresh
            stage[second, pl.ds(part * LANE, LANE), :] = fresh
        product = lax.dot_general(nrow[...], stage[second], NT, preferred_element_type=F32)
        slot, lanes = 6 + second // 2, pl.ds((second % 2) * ROWS, ROWS)
        apart[slot, :, lanes] = (product * inverse).astype(BF)
        small_copy(second).start()

    def small_copy(second):
        slot, lanes = 6 + second // 2, pl.ds((second % 2) * ROWS, ROWS)
        return remote(apart.at[slot, :, lanes], aother.at[slot, :, lanes],
                      asend.at[6 + second], arecv.at[6 + second])

    def small_cubic(second):
        small_copy(second).wait_recv()
        slot, lanes = 6 + second // 2, pl.ds((second % 2) * ROWS, ROWS)
        whole = (apart[slot, :, lanes].astype(F32) + aother[slot, :, lanes].astype(F32)).astype(BF)
        eacc[...] += lax.dot_general(whole, stage[second], NN, preferred_element_type=F32)

    def settle():
        @pl.when(y > 0)
        def _():
            from_above().wait_send()

        pltpu.make_async_copy(dbuf, dbuf, lsem.at[4]).wait()
        share(core).wait_send()
        gather_g.drain()
        gather_u.drain()
        for steps in (1, 2, 3):
            to_ring(sum_x, 0, steps, 0).wait_send()
        for slot in range(4):
            a_copy(slot).wait_send()
        small_copy(0).wait_send()
        small_copy(1).wait_send()
        wait_rows(nrow, nsem, nrecv)

    go(8)
    swap.wait()
    chip_sum = own_sum[...] + other_sum[...]
    start_ring(sum_x, 0, x, chip_sum)
    chip_norm = jnp.sqrt(jnp.maximum(jnp.sum(chip_sum), 1e-30))
    inverse = 1.0 / chip_norm
    bulk.complete(OFFSETS[0])
    go(9)
    build(0)
    gram(0)

    @pl.when(y == 0)
    def _():
        back_product()

    go(10)
    cubic(0)
    go(11)
    start_ring(sum_z, 1, z, wait_ring(sum_x, 0, x))
    bulk.complete(OFFSETS[1])
    build(1)
    go(12)
    gram(1)
    go(13)
    cubic(1)
    small(0)
    go(14)
    bulk.wait(2, 1, 0)
    small(1)
    small_cubic(0)
    bulk.wait(2, 3, 1)
    small(3)
    small_cubic(1)
    settle()
    bulk.complete(OFFSETS[2])
    build(2)
    gram(2)
    small_cubic(3)
    sum_squares = jnp.sum(wait_ring(sum_z, 1, z))
    scaling = 0.4 / jnp.sqrt(float(WIDTH) * (sum_squares / float(WIDTH * WIDTH) + 1e-06))
    bulk.wait(2, 2, 0)
    bulk.wait(2, 2, 1)
    small(2)
    cubic(2)
    small_cubic(2)
    ebf[...] = (((eacc[...] * scaling) * scaling) * (scaling * chip_norm)).astype(BF)

    for slot in (4, 5):
        a_copy(slot).wait_send()
    small_copy(2).wait_send()
    small_copy(3).wait_send()
    for steps in (1, 2, 3):
        to_ring(sum_z, 1, steps, 0).wait_send()
    for number in range(15 - DEPTH, 15):
        bulk.sent(number)

    def back_part(slot):
        product = lax.dot_general(ebf[...], nbuf[pl.ds(slot * 1024, 1024), :], NT, preferred_element_type=F32)
        fpart[slot] = (product * scaling).astype(BF)
        f_copy(slot).start()

    def back_whole(slot):
        f_copy(slot).wait_recv()
        fwhole[:, pl.ds(slot * 1024, 1024)] = (
            fpart[slot].astype(F32) + fother[slot].astype(F32)).astype(BF)

    obuf = stage.at[0]
    for slot in range(4):
        back_part(slot)
    for slot in range(3):
        back_whole(slot)
    for cut in range(4):
        lanes = pl.ds(cut * 512, 512)
        product = lax.dot_general(fwhole[:, pl.ds(0, 3072)], nbuf[pl.ds(0, 3072), lanes], NN,
                                  preferred_element_type=F32)
        if cut == 0:
            back_whole(3)
        product = product + lax.dot_general(
            fwhole[:, pl.ds(3072, 1024)], nbuf[pl.ds(3072, 1024), lanes], NN, preferred_element_type=F32)
        scaled = (nrow[:, lanes].astype(F32) * scaling).astype(BF).astype(F32)
        mixed = (quintic_a * scaled + quintic_b * ebf[:, lanes].astype(F32)
                 + quintic_c * (product * scaling))
        obuf[:, lanes] = (math.sqrt(WIDTH) * mixed).astype(BF)
        give_rows(obuf, oout, osem, orecv, lanes)

    for slot in range(4):
        f_copy(slot).wait_send()
    wait_rows(obuf, osem, orecv)


def copy_kernel(grads, fresh, update, grads_out, fresh_out, update_out, small, halves, wholes, come, leave):
    grads_in = pltpu.make_async_copy(grads, small, come.at[4])
    grads_away = pltpu.make_async_copy(small, grads_out, leave.at[4])
    arriving, leaving = [], []
    for which, (src, dst) in enumerate(((fresh, fresh_out), (update, update_out))):
        for k in range(2):
            rows, number = pl.ds(k * 64, 64), which * 2 + k
            arriving.append(pltpu.make_async_copy(src.at[:, rows], halves.at[number], come.at[number]))
            leaving.append(pltpu.make_async_copy(wholes.at[number], dst.at[0, rows], leave.at[number]))
    for one in arriving:
        one.start()
    grads_in.start()
    for number in range(4):
        arriving[number].wait()
        for k in range(CHIPS):
            for half in range(2):
                wholes[number, :, (2 * k + half) * LANE:(2 * k + half + 1) * LANE] = (
                    halves[number, half, :, k * LANE:(k + 1) * LANE])
        leaving[number].start()
    grads_in.wait()
    grads_away.start()
    for one in leaving:
        one.wait()
    grads_away.wait()


def per_device(cotangent, stashed_inputs, weights, momentum):
    anywhere = pl.BlockSpec(memory_space=pl.ANY)
    sem = pltpu.SemaphoreType.DMA
    scratch = [
        pltpu.VMEM((WIDTH, HALF), BF),
        pltpu.VMEM((WIDTH, HALF), BF),
        pltpu.VMEM((ROWS, HALF), BF),
        pltpu.VMEM((2, LANE, HALF), BF),
        pltpu.VMEM((TOKENS, HALF), BF),
        pltpu.VMEM((2, HALF, TOKENS), BF),
        pltpu.VMEM((2, LANE, LANE), BF),
        pltpu.VMEM((TOKENS, LANE), F32),
        pltpu.VMEM((TOKENS, LANE), BF),
        pltpu.VMEM((TOKENS, LANE), F32),
        pltpu.VMEM((TOKENS, LANE), F32),
        pltpu.VMEM((TOKENS, LANE), F32),
        pltpu.VMEM((8, ROWS, 512), BF),
        pltpu.VMEM((8, ROWS, 512), BF),
        pltpu.VMEM((4, ROWS, 1024), BF),
        pltpu.VMEM((4, ROWS, 1024), BF),
        pltpu.VMEM((ROWS, HALF), F32),
        pltpu.VMEM((ROWS, HALF), BF),
        pltpu.VMEM((ROWS, WIDTH), BF),
        pltpu.VMEM((RING, ROWS, HALF), BF),
        pltpu.VMEM((8, LANE), F32),
        pltpu.VMEM((8, LANE), F32),
        pltpu.VMEM((RING, 8, LANE), F32),
        pltpu.VMEM((RING, 8, LANE), F32),
        sem((5,)),
        sem((6,)),
        sem((6,)),
        sem((60,)),
        sem((2, CHIPS, 2)),
        sem((30,)),
        sem((2, CHIPS)),
        sem((30,)),
        sem((2, CHIPS)),
        sem((10,)),
        sem((10,)),
        sem((4,)),
        sem((4,)),
        sem((2,)),
        sem,
        sem((2,)),
        sem,
        sem((2, 3)),
        sem((2, RING)),
    ]
    held = pl.pallas_call(
        step_kernel,
        out_shape=(
            jax.ShapeDtypeStruct(stashed_inputs.shape, BF),
            jax.ShapeDtypeStruct((2, LANE, HALF), BF),
            jax.ShapeDtypeStruct((2, LANE, HALF), BF),
        ),
        in_specs=[anywhere] * 4,
        out_specs=(anywhere, anywhere, anywhere),
        scratch_shapes=scratch,
        compiler_params=pltpu.CompilerParams(
            collective_id=0, has_side_effects=True, vmem_limit_bytes=62 * 1024 * 1024),
        cost_estimate=pl.CostEstimate(
            flops=22 * 10**9, bytes_accessed=6 * 2**20, transcendentals=32768),
    )(cotangent, stashed_inputs, weights, momentum)
    return pl.pallas_call(
        copy_kernel,
        out_shape=(
            jax.ShapeDtypeStruct(stashed_inputs.shape, BF),
            jax.ShapeDtypeStruct(momentum.shape, BF),
            jax.ShapeDtypeStruct(momentum.shape, BF),
        ),
        in_specs=[anywhere] * 3,
        out_specs=(anywhere, anywhere, anywhere),
        scratch_shapes=[
            pltpu.VMEM((1, 2, LANE, LANE), BF), pltpu.VMEM((4, 2, 64, HALF), BF),
            pltpu.VMEM((4, 64, WIDTH), BF), sem((5,)), sem((5,))],
    )(*held)


def solution(mesh):
    in_specs = (
        P(None, None, "dp"),
        P("pipe", None, None, "dp"),
        P("pipe", "dp", None),
        P("pipe", "dp", None),
    )
    out_specs = (P("pipe", None, None, "dp"), P("pipe", "dp", None), P("pipe", "dp", None))
    return jax.shard_map(
        per_device, mesh=mesh, in_specs=in_specs, out_specs=out_specs, check_vma=False
    )
```

```python
import functools
import math

import jax
import jax.numpy as jnp
from jax import lax
from jax.experimental import pallas as pl
from jax.experimental.pallas import tpu as pltpu
from jax.sharding import PartitionSpec as P

quintic_a = 3.4445
quintic_b = -4.775
quintic_c = 2.0315

MESH = pl.DeviceIdType.MESH
BF = jnp.bfloat16
F32 = jnp.float32
RING = 4
CHIPS = 16
LANE = 128
WIDTH = 4096
HALF = 2048
TOKENS = 256
ROWS = 256
OFFSETS = (0, 1, 3, 2)
NT = (((1,), (1,)), ((), ()))
NN = (((1,), (0,)), ((), ()))


def place():
    spot = lax.axis_index("dp")
    return lax.axis_index("pipe"), spot // 8, (spot // 2) % RING, spot % 2


def at(y, z, x, core):
    return (y, ((z % RING) * RING + x % RING) * 2 + core)


def chip_of(z, x):
    return (z % RING) * RING + x % RING


def multiple(value, of):
    return pl.multiple_of(value, of)


def offset_of(index):
    return index + (index // 2) * (5 - 2 * index)


def ring(value, steps):
    return (value + steps) % RING


class Plane:
    def __init__(self):
        self.y, self.z, self.x, self.core = place()
        self.sibling = at(self.y, self.z, self.x, 1 - self.core)

    def own(self, part):
        return (self.x, self.z) if part == 0 else (self.z, self.x)

    def spot(self, part, first, second):
        own_first, own_second = self.own(part)
        return ring(own_first, first), ring(own_second, second)

    def target(self, part, axis, steps):
        along_x = (axis == 0) == (part == 0)
        if along_x:
            return at(self.y, self.z, self.x + steps, self.core)
        return at(self.y, self.z + steps, self.x, self.core)

    def remote(self, src, dst, send_sem, recv_sem, device=None):
        return pltpu.make_async_remote_copy(
            src_ref=src, dst_ref=dst, send_sem=send_sem, recv_sem=recv_sem,
            device_id=self.sibling if device is None else device, device_id_type=MESH,
        )


class TwoStage:
    def __init__(self, plane, slot, send, recv):
        self.plane, self.slot, self.send, self.recv = plane, slot, send, recv

    def copy(self, part, first, second, axis, steps, number):
        one, two = self.plane.spot(part, first, second)
        z, x = (two, one) if part == 0 else (one, two)
        ref = self.slot(z, x, part)
        return self.plane.remote(ref, ref, self.send.at[number], self.recv.at[part, one * RING + two],
                                 self.plane.target(part, axis, steps))

    def wait(self, part, first, second):
        self.copy(part, first, second, 0, 1, 0).wait_recv()

    def start(self):
        number = 0
        for axis in (0, 1):
            for steps in (1, 3, 2):
                for part in (0, 1):
                    self.copy(part, 0, 0, axis, steps, number).start()
                    number += 1

    def forward(self):
        number = 12
        for first in (1, 3, 2):
            for part in (0, 1):
                self.wait(part, first, 0)
                for steps in (1, 3, 2):
                    self.copy(part, first, 0, 1, steps, number).start()
                    number += 1

    def finish(self):
        for first in (0, 1, 3, 2):
            for part in (0, 1):
                for second in (1, 3, 2):
                    self.wait(part, first, second)

    def drain(self):
        def body(number, carry):
            self.copy(0, 0, 0, 0, 1, number).wait_send()
            return carry

        lax.fori_loop(0, 30, body, 0)


DEPTH = 2
CHUNKS = ((0, 1), (2, 3, 4), (5, 6, 7))
EXTRA = {3: (0, 1), 2: (2, 3), 1: (5,), 0: (8,)}


class Bulk:
    def __init__(self, plane, buf, send, recv):
        self.plane, self.buf, self.send, self.recv = plane, buf, send, recv

    def copy(self, part, first, second, half, axis, steps, number):
        one, two = self.plane.spot(part, first, second)
        row = part * HALF + (one * RING + two) * LANE + half * 64
        ref = self.buf.at[pl.ds(multiple(row, 64), 64), :]
        return self.plane.remote(ref, ref, self.send.at[number], self.recv.at[part, one * RING + two, half],
                                 self.plane.target(part, axis, steps))

    def wait(self, first, second, half):
        for part in (0, 1):
            self.copy(part, first, second, half, 0, 1, 0).wait_recv()

    def sent(self, number):
        for k in range(4):
            self.copy(0, 0, 0, 0, 0, 1, number * 4 + k).wait_send()

    def put(self, number, plus, minus, axis):
        if number >= DEPTH:
            self.sent(number - DEPTH)
        for k, (what, steps) in enumerate(((plus, 1), (minus, 3))):
            for part in (0, 1):
                self.copy(part, *what, axis, steps, number * 4 + k * 2 + part).start()

    def spread(self, number, first, half):
        self.put(number, (first, 0, half), (first, 0, half), 1)

    def pass_on(self, number, first):
        self.wait(first, 3, 0)
        self.wait(first, 1, 1)
        self.put(number, (first, 3, 0), (first, 1, 1), 1)

    def round(self, number):
        if number < 2:
            self.put(number, (0, 0, number), (0, 0, number), 0)
        elif number < 4:
            self.spread(number, 0, number - 2)
        elif number == 4:
            self.wait(3, 0, 0)
            self.wait(1, 0, 1)
            self.put(number, (3, 0, 0), (1, 0, 1), 0)
        elif number == 5:
            self.wait(1, 0, 0)
            self.spread(number, 1, 0)
        elif number == 6:
            self.spread(number, 1, 1)
        elif number == 7:
            self.pass_on(number, 0)
        elif number == 8:
            self.spread(number, 3, 0)
        elif number == 9:
            self.wait(3, 0, 1)
            self.spread(number, 3, 1)
        elif number == 10:
            self.pass_on(number, 1)
        elif number in (11, 12):
            self.wait(2, 0, number - 11)
            self.spread(number, 2, number - 11)
        elif number == 13:
            self.pass_on(number, 3)
        elif number == 14:
            self.pass_on(number, 2)

    def complete(self, first):
        self.wait(first, 1, 0)
        self.wait(first, 3, 1)
        self.wait(first, 2, 0)
        self.wait(first, 2, 1)


def step_kernel(
    cot, xs, w, m, dout, nout, oout,
    mbuf, nbuf, nrow, wbuf, ubuf, gbuf, xin, slope, dbuf, bsend, brecv, bown, apart, aother, fother,
    eacc, ebf, stage, own_sum, other_sum, sum_x, sum_z,
    lsem, sib_send, sib_recv, msend, mrecv, gsend, grecv, usend, urecv,
    asend, arecv, fsend, frecv, osem, orecv, nsem, nrecv, ssend, srecv,
):
    plane = Plane()
    y, z, x, core = plane.y, plane.z, plane.x, plane.core
    remote = plane.remote
    me = chip_of(z, x)
    own_spot = (1 - core) * (x * RING + z) + core * (z * RING + x)

    partners = [at(y, z, x + 1, core), at(y, z, x + 2, core), at(y, z, x + 3, core),
                at(y, z + 1, x, core), at(y, z + 2, x, core), at(y, z + 3, x, core),
                plane.sibling, at(ring(y, 1), z, x, core), at(ring(y, 3), z, x, core)]
    load_x = pltpu.make_async_copy(xs.at[0], xin, lsem.at[0])
    own_u = ubuf.at[:, pl.ds(multiple(me * LANE, LANE), LANE)]
    barrier = pltpu.get_barrier_semaphore()
    for partner in partners:
        pl.semaphore_signal(barrier, 1, device_id=partner, device_id_type=MESH)

    @pl.when(y == RING - 1)
    def _():
        for micro in range(2):
            pltpu.make_async_copy(
                cot.at[micro],
                ubuf.at[pl.ds(micro * LANE, LANE), pl.ds(multiple(me * LANE, LANE), LANE)],
                lsem.at[3]).start()

    load_x.start()
    own_m = mbuf.at[pl.ds(multiple(core * HALF + own_spot * LANE, LANE), LANE), :]

    def load_rows(src, at_stage, which):
        for half in (0, 1):
            pltpu.make_async_copy(src.at[0, :, pl.ds(half * HALF, HALF)],
                                  stage.at[at_stage, pl.ds(half * LANE, LANE), :], lsem.at[which]).start()

    def given(at_stage, dst, which):
        return remote(stage.at[at_stage + 1, pl.ds(0, LANE), :], dst, sib_send.at[which], sib_recv.at[which])

    def split_rows(at_stage, dst, which, own_which):
        whole = stage.at[at_stage]
        pltpu.make_async_copy(whole, whole, lsem.at[own_which]).wait()
        for k in range(CHIPS):
            half, lanes = k // 8, pl.ds(k * LANE, LANE)
            for mine in (1, 0):
                which_core = core if mine else 1 - core
                source = pl.ds(multiple((2 * (k % 8) + which_core) * LANE, LANE), LANE)
                piece = stage[at_stage, pl.ds(half * LANE, LANE), source]
                if mine:
                    dst[:, lanes] = piece
                else:
                    stage[at_stage + 1, pl.ds(0, LANE), lanes] = piece
        given(at_stage, dst, which).start()

    load_rows(m, 0, 1)
    load_rows(w, 2, 2)
    pl.semaphore_wait(barrier, len(partners))

    def u_slot(z_at, x_at, part):
        return ubuf.at[pl.ds(part * LANE, LANE), pl.ds(multiple((z_at * RING + x_at) * LANE, LANE), LANE)]

    gather_u = TwoStage(plane, u_slot, usend, urecv)

    @pl.when(y == RING - 1)
    def _():
        pltpu.make_async_copy(own_u, own_u, lsem.at[3]).wait()
        gather_u.start()

    split_rows(0, own_m, 0, 1)

    load_x.wait()
    values = xin[...].reshape(TOKENS, LANE).astype(F32)
    sigmoid_val = jax.nn.sigmoid(values)
    slope[...] = sigmoid_val * (1.0 + values * (1.0 - sigmoid_val))
    gated = (values * sigmoid_val).astype(BF).astype(F32)
    gbuf[core, pl.ds(multiple(own_spot * LANE, LANE), LANE), :] = jnp.transpose(gated).astype(BF)

    def load_weights():
        split_rows(2, wbuf.at[core], 1, 2)

    def g_slot(z_at, x_at, part):
        spot = (1 - core) * (x_at * RING + z_at) + core * (z_at * RING + x_at)
        return gbuf.at[core, pl.ds(multiple(spot * LANE + part * 64, 64), 64), :]

    bulk = Bulk(plane, mbuf, msend, mrecv)
    gather_g = TwoStage(plane, g_slot, gsend, grecv)

    def from_above():
        return remote(dbuf, own_u, sib_send.at[3], sib_recv.at[3], at(ring(y, 3), z, x, core))

    def own_rows_here():
        given(0, own_m, 0).wait()

    def go(number):
        taken = [at_y for at_y, rounds in EXTRA.items() if number in rounds]
        if not taken:
            bulk.round(number)
        else:
            @pl.when(y != taken[0])
            def _():
                bulk.round(number)

    def chain():
        @pl.when(y < RING - 1)
        def _():
            from_above().wait_recv()
            gather_u.start()

        gather_u.forward()
        for at_y, rounds in EXTRA.items():
            @pl.when(y == at_y)
            def _(rounds=rounds, at_y=at_y):
                if at_y == RING - 1:
                    gather_g.start()
                    own_rows_here()
                    load_weights()
                for number in rounds:
                    bulk.round(number)

        gather_u.finish()

        @pl.when(y > 0)
        def _():
            back_product()

    def back_product():
        given(2, wbuf.at[core], 1).wait()
        full = ubuf[...]
        bsend[...] = lax.dot_general(full, wbuf[1 - core], NT, preferred_element_type=F32)
        give = remote(bsend, brecv, sib_send.at[2], sib_recv.at[2])
        give.start()
        bown[...] = lax.dot_general(full, wbuf[core], NT, preferred_element_type=F32)
        give.wait()
        back = bown[...] + brecv[...]
        upstream = ubuf[:, pl.ds(multiple(me * LANE, LANE), LANE)].astype(F32)
        dbuf[...] = (upstream + slope[...] * back).astype(BF)

        @pl.when(y > 0)
        def _():
            from_above().start()

        for micro in range(2):
            pltpu.make_async_copy(
                dbuf.at[pl.ds(micro * LANE, LANE), :], dout.at[0, micro], lsem.at[4]).start()

    def front(index, carry):
        @pl.when(index == RING - 1 - y)
        def _():
            chain()

        for which, rounds in enumerate(CHUNKS):
            @pl.when(index == which)
            def _(which=which, rounds=rounds):
                if which == 0:
                    @pl.when(y < RING - 1)
                    def _():
                        gather_g.start()
                        own_rows_here()
                        load_weights()
                if which == 1:
                    gather_g.forward()
                for number in rounds:
                    go(number)
        return carry

    lax.fori_loop(0, RING, front, 0)

    def share(part):
        return remote(gbuf.at[part], gbuf.at[part], sib_send.at[4], sib_recv.at[4])

    gather_g.finish()
    share(core).start()

    share(1 - core).wait_recv()
    sums = jnp.zeros((8, LANE), F32)
    for part in (0, 1):
        one, two = plane.own(part)
        spot = one * RING + two
        grad = lax.dot_general(
            gbuf[part, pl.ds(multiple(spot * LANE, LANE), LANE), :], ubuf[...], NN,
            preferred_element_type=F32)
        old = mbuf[pl.ds(multiple(part * HALF + spot * LANE, LANE), LANE), :].astype(F32)
        fresh = (0.95 * old + grad).astype(BF)
        nrow[pl.ds(part * LANE, LANE), :] = fresh
        wide = fresh.astype(F32)
        square = wide * wide
        for k in range(CHIPS):
            sums = sums + jnp.sum(
                square[:, k * LANE:(k + 1) * LANE].reshape(16, 8, LANE), axis=0)
    own_sum[...] = sums
    swap = remote(own_sum, other_sum, sib_send.at[5], sib_recv.at[5])
    swap.start()

    def give_rows(buf, out, sem, recv, lanes=pl.ds(0, HALF)):
        pltpu.make_async_copy(
            buf.at[pl.ds(multiple(core * LANE, LANE), LANE), lanes], out.at[core, :, lanes], sem.at[0]).start()
        remote(buf.at[pl.ds(multiple((1 - core) * LANE, LANE), LANE), lanes], out.at[core, :, lanes],
               sem.at[1], recv).start()

    def wait_rows(buf, sem, recv):
        half = buf.at[pl.ds(0, LANE), :]
        pltpu.make_async_copy(half, half, sem.at[0]).wait()
        both = remote(half, half, sem.at[1], recv)
        both.wait_send()
        both.wait_recv()

    give_rows(nrow, nout, nsem, nrecv)

    def to_ring(buf, axis, steps, own):
        return remote(buf.at[own], buf.at[own], ssend.at[axis, steps - 1], srecv.at[axis, own],
                      plane.target(0, axis, steps))

    def start_ring(buf, axis, own, value):
        buf[own] = value
        for steps in (1, 2, 3):
            to_ring(buf, axis, steps, own).start()

    def wait_ring(buf, axis, own):
        for steps in (1, 2, 3):
            to_ring(buf, axis, steps, ring(own, steps)).wait_recv()
        return buf[0] + buf[1] + buf[2] + buf[3]

    def own_first(part):
        return x + part * (z - x)

    def own_second(part):
        return z + part * (x - z)

    def group_rows(index, part):
        return multiple(ring(own_first(part), offset_of(index)) * 512, 512)

    def both_parts(body):
        def one(part, carry):
            body(part)
            return carry

        lax.fori_loop(0, 2, one, 0)

    def slot_lanes(slot, width):
        return pl.ds(multiple(slot * width, width), width)

    fpart, fwhole = apart, aother

    def a_copy(slot):
        lanes = slot_lanes(slot, 512)
        return remote(apart.at[:, lanes], aother.at[:, lanes], asend.at[slot], arecv.at[slot])

    def f_copy(slot):
        lanes = slot_lanes(slot, 1024)
        return remote(fpart.at[:, lanes], fother.at[:, lanes], fsend.at[slot], frecv.at[slot])

    def build_and_gram(index):
        def body(part):
            start = group_rows(index, part)
            rows = pl.ds(multiple(part * HALF + start, 512), 512)
            grad = lax.dot_general(gbuf[part, pl.ds(start, 512), :], ubuf[...], NN,
                                   preferred_element_type=F32)
            nbuf[rows, :] = (0.95 * mbuf[rows, :].astype(F32) + grad).astype(BF)
            product = lax.dot_general(nrow[...], nbuf[rows, :], NT, preferred_element_type=F32)
            apart[:, slot_lanes(index * 2 + part, 512)] = (product * inverse).astype(BF)
            a_copy(index * 2 + part).start()

        both_parts(body)

    def cubic(index):
        def body(part):
            rows = pl.ds(multiple(part * HALF + group_rows(index, part), 512), 512)
            slot = index * 2 + part
            a_copy(slot).wait_recv()
            lanes = slot_lanes(slot, 512)
            whole = (apart[:, lanes].astype(F32) + aother[:, lanes].astype(F32)).astype(BF)
            eacc[...] += lax.dot_general(whole, nbuf[rows, :], NN, preferred_element_type=F32)

        both_parts(body)

    def small(second):
        def body(part):
            first, last = ring(own_first(part), OFFSETS[3]), ring(own_second(part), second)
            start = multiple((first * RING + last) * LANE, LANE)
            rows = pl.ds(multiple(part * HALF + start, LANE), LANE)
            grad = lax.dot_general(gbuf[part, pl.ds(start, LANE), :], ubuf[...], NN,
                                   preferred_element_type=F32)
            fresh = (0.95 * mbuf[rows, :].astype(F32) + grad).astype(BF)
            nbuf[rows, :] = fresh
            stage[second, pl.ds(multiple(part * LANE, LANE), LANE), :] = fresh

        both_parts(body)
        product = lax.dot_general(nrow[...], stage[second], NT, preferred_element_type=F32)
        lanes = slot_lanes(12 + second, ROWS)
        apart[:, lanes] = (product * inverse).astype(BF)
        small_copy(second).start()

    def small_copy(second):
        lanes = slot_lanes(12 + second, ROWS)
        return remote(apart.at[:, lanes], aother.at[:, lanes],
                      asend.at[6 + second], arecv.at[6 + second])

    def small_cubic(second):
        small_copy(second).wait_recv()
        lanes = slot_lanes(12 + second, ROWS)
        whole = (apart[:, lanes].astype(F32) + aother[:, lanes].astype(F32)).astype(BF)
        eacc[...] += lax.dot_general(whole, stage[second], NN, preferred_element_type=F32)

    def settle():
        @pl.when(y > 0)
        def _():
            from_above().wait_send()

        pltpu.make_async_copy(dbuf, dbuf, lsem.at[4]).wait()
        share(core).wait_send()
        gather_g.drain()
        gather_u.drain()
        for steps in (1, 2, 3):
            to_ring(sum_x, 0, steps, 0).wait_send()
        for slot in range(4):
            a_copy(slot).wait_send()
        small_copy(0).wait_send()
        small_copy(1).wait_send()
        wait_rows(nrow, nsem, nrecv)

    go(8)
    swap.wait()
    chip_sum = own_sum[...] + other_sum[...]
    start_ring(sum_x, 0, x, chip_sum)
    chip_norm = jnp.sqrt(jnp.maximum(jnp.sum(chip_sum), 1e-30))
    inverse = 1.0 / chip_norm
    eacc[...] = jnp.zeros_like(eacc)

    def stream(index, carry):
        @pl.when(index == 2)
        def _():
            def pieces(k, carry):
                second = offset_of(k)

                @pl.when(k == 1)
                def _():
                    bulk.wait(2, 1, 0)

                @pl.when(k == 2)
                def _():
                    bulk.wait(2, 3, 1)

                small(second)

                @pl.when(k > 0)
                def _():
                    small_cubic(offset_of(k - 1))

                return carry

            lax.fori_loop(0, 3, pieces, 0)
            settle()

        bulk.complete(offset_of(index))

        @pl.when(index == 0)
        def _():
            go(9)

        build_and_gram(index)

        @pl.when(index == 0)
        def _():
            @pl.when(y == 0)
            def _():
                back_product()

            go(10)

        @pl.when(index == 1)
        def _():
            go(12)

        cubic(index)

        @pl.when(index == 0)
        def _():
            go(11)
            start_ring(sum_z, 1, z, wait_ring(sum_x, 0, x))

        @pl.when(index == 1)
        def _():
            go(13)
            go(14)

        return carry

    lax.fori_loop(0, 3, stream, 0)
    sum_squares = jnp.sum(wait_ring(sum_z, 1, z))
    scaling = 0.4 / jnp.sqrt(float(WIDTH) * (sum_squares / float(WIDTH * WIDTH) + 1e-06))
    bulk.wait(2, 2, 0)
    bulk.wait(2, 2, 1)
    small(2)

    def last_pieces(k, carry):
        small_cubic(offset_of(k))
        return carry

    lax.fori_loop(2, 4, last_pieces, 0)
    ebf[...] = (((eacc[...] * scaling) * scaling) * (scaling * chip_norm)).astype(BF)

    for slot in (4, 5):
        a_copy(slot).wait_send()
    small_copy(2).wait_send()
    small_copy(3).wait_send()
    obuf = stage.at[0]

    def all_back(slot, carry):
        product = lax.dot_general(ebf[...], nbuf[pl.ds(multiple(slot * 1024, 1024), 1024), :], NT,
                                  preferred_element_type=F32)
        fpart[:, slot_lanes(slot, 1024)] = (product * scaling).astype(BF)
        f_copy(slot).start()
        return carry

    lax.fori_loop(0, 4, all_back, 0)

    def back_whole(slot):
        f_copy(slot).wait_recv()
        lanes = slot_lanes(slot, 1024)
        fwhole[:, lanes] = (fpart[:, lanes].astype(F32) + fother[:, lanes].astype(F32)).astype(BF)

    for slot in range(3):
        back_whole(slot)

    def cuts(cut, carry):
        lanes = pl.ds(multiple(cut * 512, 512), 512)
        product = lax.dot_general(fwhole[:, pl.ds(0, 3072)], nbuf[pl.ds(0, 3072), lanes], NN,
                                  preferred_element_type=F32)

        @pl.when(cut == 0)
        def _():
            back_whole(3)

        product = product + lax.dot_general(
            fwhole[:, pl.ds(3072, 1024)], nbuf[pl.ds(3072, 1024), lanes], NN, preferred_element_type=F32)
        scaled = (nrow[:, lanes].astype(F32) * scaling).astype(BF).astype(F32)
        mixed = (quintic_a * scaled + quintic_b * ebf[:, lanes].astype(F32)
                 + quintic_c * (product * scaling))
        obuf[:, lanes] = (math.sqrt(WIDTH) * mixed).astype(BF)
        give_rows(obuf, oout, osem, orecv, lanes)
        return carry

    lax.fori_loop(0, 4, cuts, 0)

    for steps in (1, 2, 3):
        to_ring(sum_z, 1, steps, 0).wait_send()
    for number in range(15 - DEPTH, 15):
        bulk.sent(number)
    for slot in range(4):
        f_copy(slot).wait_send()
    wait_rows(obuf, osem, orecv)


def copy_kernel(grads, fresh, update, grads_out, fresh_out, update_out, small, halves, wholes, come, leave):
    grads_in = pltpu.make_async_copy(grads, small, come.at[4])
    grads_away = pltpu.make_async_copy(small, grads_out, leave.at[4])
    arriving, leaving = [], []
    for which, (src, dst) in enumerate(((fresh, fresh_out), (update, update_out))):
        for k in range(2):
            rows, number = pl.ds(k * 64, 64), which * 2 + k
            arriving.append(pltpu.make_async_copy(src.at[:, rows], halves.at[number], come.at[number]))
            leaving.append(pltpu.make_async_copy(wholes.at[number], dst.at[0, rows], leave.at[number]))
    for one in arriving:
        one.start()
    grads_in.start()
    for number in range(4):
        arriving[number].wait()
        for k in range(CHIPS):
            for half in range(2):
                wholes[number, :, (2 * k + half) * LANE:(2 * k + half + 1) * LANE] = (
                    halves[number, half, :, k * LANE:(k + 1) * LANE])
        leaving[number].start()
    grads_in.wait()
    grads_away.start()
    for one in leaving:
        one.wait()
    grads_away.wait()


def per_device(cotangent, stashed_inputs, weights, momentum):
    anywhere = pl.BlockSpec(memory_space=pl.ANY)
    sem = pltpu.SemaphoreType.DMA
    scratch = [
        pltpu.VMEM((WIDTH, HALF), BF),
        pltpu.VMEM((WIDTH, HALF), BF),
        pltpu.VMEM((ROWS, HALF), BF),
        pltpu.VMEM((2, LANE, HALF), BF),
        pltpu.VMEM((TOKENS, HALF), BF),
        pltpu.VMEM((2, HALF, TOKENS), BF),
        pltpu.VMEM((2, LANE, LANE), BF),
        pltpu.VMEM((TOKENS, LANE), F32),
        pltpu.VMEM((TOKENS, LANE), BF),
        pltpu.VMEM((TOKENS, LANE), F32),
        pltpu.VMEM((TOKENS, LANE), F32),
        pltpu.VMEM((TOKENS, LANE), F32),
        pltpu.VMEM((ROWS, WIDTH), BF),
        pltpu.VMEM((ROWS, WIDTH), BF),
        pltpu.VMEM((ROWS, WIDTH), BF),
        pltpu.VMEM((ROWS, HALF), F32),
        pltpu.VMEM((ROWS, HALF), BF),
        pltpu.VMEM((RING, ROWS, HALF), BF),
        pltpu.VMEM((8, LANE), F32),
        pltpu.VMEM((8, LANE), F32),
        pltpu.VMEM((RING, 8, LANE), F32),
        pltpu.VMEM((RING, 8, LANE), F32),
        sem((5,)),
        sem((6,)),
        sem((6,)),
        sem((60,)),
        sem((2, CHIPS, 2)),
        sem((30,)),
        sem((2, CHIPS)),
        sem((30,)),
        sem((2, CHIPS)),
        sem((10,)),
        sem((10,)),
        sem((4,)),
        sem((4,)),
        sem((2,)),
        sem,
        sem((2,)),
        sem,
        sem((2, 3)),
        sem((2, RING)),
    ]
    held = pl.pallas_call(
        step_kernel,
        out_shape=(
            jax.ShapeDtypeStruct(stashed_inputs.shape, BF),
            jax.ShapeDtypeStruct((2, LANE, HALF), BF),
            jax.ShapeDtypeStruct((2, LANE, HALF), BF),
        ),
        in_specs=[anywhere] * 4,
        out_specs=(anywhere, anywhere, anywhere),
        scratch_shapes=scratch,
        compiler_params=pltpu.CompilerParams(
            collective_id=0, has_side_effects=True, vmem_limit_bytes=62 * 1024 * 1024),
        cost_estimate=pl.CostEstimate(
            flops=22 * 10**9, bytes_accessed=6 * 2**20, transcendentals=32768),
    )(cotangent, stashed_inputs, weights, momentum)
    return pl.pallas_call(
        copy_kernel,
        out_shape=(
            jax.ShapeDtypeStruct(stashed_inputs.shape, BF),
            jax.ShapeDtypeStruct(momentum.shape, BF),
            jax.ShapeDtypeStruct(momentum.shape, BF),
        ),
        in_specs=[anywhere] * 3,
        out_specs=(anywhere, anywhere, anywhere),
        scratch_shapes=[
            pltpu.VMEM((1, 2, LANE, LANE), BF), pltpu.VMEM((4, 2, 64, HALF), BF),
            pltpu.VMEM((4, 64, WIDTH), BF), sem((5,)), sem((5,))],
    )(*held)


def solution(mesh):
    in_specs = (
        P(None, None, "dp"),
        P("pipe", None, None, "dp"),
        P("pipe", "dp", None),
        P("pipe", "dp", None),
    )
    out_specs = (P("pipe", None, None, "dp"), P("pipe", "dp", None), P("pipe", "dp", None))
    return jax.shard_map(
        per_device, mesh=mesh, in_specs=in_specs, out_specs=out_specs, check_vma=False
    )
```

```python
import functools
import math

import jax
import jax.numpy as jnp
from jax import lax
from jax.experimental import pallas as pl
from jax.experimental.pallas import tpu as pltpu
from jax.sharding import PartitionSpec as P

quintic_a = 3.4445
quintic_b = -4.775
quintic_c = 2.0315

MESH = pl.DeviceIdType.MESH
BF = jnp.bfloat16
F32 = jnp.float32
RING = 4
CHIPS = 16
LANE = 128
WIDTH = 4096
HALF = 2048
TOKENS = 256
ROWS = 256
OFFSETS = (0, 1, 3, 2)
NT = (((1,), (1,)), ((), ()))
NN = (((1,), (0,)), ((), ()))


def place():
    spot = lax.axis_index("dp")
    return lax.axis_index("pipe"), spot // 8, (spot // 2) % RING, spot % 2


def at(y, z, x, core):
    return (y, ((z % RING) * RING + x % RING) * 2 + core)


def chip_of(z, x):
    return (z % RING) * RING + x % RING


def multiple(value, of):
    return pl.multiple_of(value, of)


def offset_of(index):
    return index + (index // 2) * (5 - 2 * index)


def ring(value, steps):
    return (value + steps) % RING


class Plane:
    def __init__(self):
        self.y, self.z, self.x, self.core = place()
        self.sibling = at(self.y, self.z, self.x, 1 - self.core)

    def own(self, part):
        return (self.x, self.z) if part == 0 else (self.z, self.x)

    def spot(self, part, first, second):
        own_first, own_second = self.own(part)
        return ring(own_first, first), ring(own_second, second)

    def target(self, part, axis, steps):
        along_x = (axis == 0) == (part == 0)
        if along_x:
            return at(self.y, self.z, self.x + steps, self.core)
        return at(self.y, self.z + steps, self.x, self.core)

    def remote(self, src, dst, send_sem, recv_sem, device=None):
        return pltpu.make_async_remote_copy(
            src_ref=src, dst_ref=dst, send_sem=send_sem, recv_sem=recv_sem,
            device_id=self.sibling if device is None else device, device_id_type=MESH,
        )


class TwoStage:
    def __init__(self, plane, slot, send, recv):
        self.plane, self.slot, self.send, self.recv = plane, slot, send, recv

    def copy(self, part, first, second, axis, steps, number):
        one, two = self.plane.spot(part, first, second)
        z, x = (two, one) if part == 0 else (one, two)
        ref = self.slot(z, x, part)
        return self.plane.remote(ref, ref, self.send.at[number], self.recv.at[part, one * RING + two],
                                 self.plane.target(part, axis, steps))

    def wait(self, part, first, second):
        self.copy(part, first, second, 0, 1, 0).wait_recv()

    def start(self):
        number = 0
        for axis in (0, 1):
            for steps in (1, 3, 2):
                for part in (0, 1):
                    self.copy(part, 0, 0, axis, steps, number).start()
                    number += 1

    def forward(self):
        number = 12
        for first in (1, 3, 2):
            for part in (0, 1):
                self.wait(part, first, 0)
                for steps in (1, 3, 2):
                    self.copy(part, first, 0, 1, steps, number).start()
                    number += 1

    def finish(self):
        for first in (0, 1, 3, 2):
            for part in (0, 1):
                for second in (1, 3, 2):
                    self.wait(part, first, second)

    def drain(self):
        def body(number, carry):
            self.copy(0, 0, 0, 0, 1, number).wait_send()
            return carry

        lax.fori_loop(0, 30, body, 0)


DEPTH = 2
CHUNKS = ((0, 1), (2, 3, 4), (5, 6, 7))
EXTRA = {3: (0, 1), 2: (2, 3), 1: (5,), 0: (8, 9)}


class Bulk:
    def __init__(self, plane, buf, send, recv):
        self.plane, self.buf, self.send, self.recv = plane, buf, send, recv

    def copy(self, part, first, second, half, axis, steps, number):
        one, two = self.plane.spot(part, first, second)
        row = part * HALF + (one * RING + two) * LANE + half * 64
        ref = self.buf.at[pl.ds(multiple(row, 64), 64), :]
        return self.plane.remote(ref, ref, self.send.at[number], self.recv.at[part, one * RING + two, half],
                                 self.plane.target(part, axis, steps))

    def wait(self, first, second, half):
        for part in (0, 1):
            self.copy(part, first, second, half, 0, 1, 0).wait_recv()

    def sent(self, number):
        for k in range(4):
            self.copy(0, 0, 0, 0, 0, 1, number * 4 + k).wait_send()

    def put(self, number, plus, minus, axis):
        if number >= DEPTH:
            self.sent(number - DEPTH)
        for k, (what, steps) in enumerate(((plus, 1), (minus, 3))):
            for part in (0, 1):
                self.copy(part, *what, axis, steps, number * 4 + k * 2 + part).start()

    def spread(self, number, first, half):
        self.put(number, (first, 0, half), (first, 0, half), 1)

    def pass_on(self, number, first):
        self.wait(first, 3, 0)
        self.wait(first, 1, 1)
        self.put(number, (first, 3, 0), (first, 1, 1), 1)

    def round(self, number):
        if number < 2:
            self.put(number, (0, 0, number), (0, 0, number), 0)
        elif number < 4:
            self.spread(number, 0, number - 2)
        elif number == 4:
            self.wait(3, 0, 0)
            self.wait(1, 0, 1)
            self.put(number, (3, 0, 0), (1, 0, 1), 0)
        elif number == 5:
            self.wait(1, 0, 0)
            self.spread(number, 1, 0)
        elif number == 6:
            self.spread(number, 1, 1)
        elif number == 7:
            self.pass_on(number, 0)
        elif number == 8:
            self.spread(number, 3, 0)
        elif number == 9:
            self.wait(3, 0, 1)
            self.spread(number, 3, 1)
        elif number == 10:
            self.pass_on(number, 1)
        elif number in (11, 12):
            self.wait(2, 0, number - 11)
            self.spread(number, 2, number - 11)
        elif number == 13:
            self.pass_on(number, 3)
        elif number == 14:
            self.pass_on(number, 2)

    def complete(self, first):
        self.wait(first, 1, 0)
        self.wait(first, 3, 1)
        self.wait(first, 2, 0)
        self.wait(first, 2, 1)


def step_kernel(
    cot, xs, w, m, dout, nout, oout,
    mbuf, nbuf, nrow, wbuf, ubuf, gbuf, xin, slope, dbuf, bsend, brecv, bown, apart, aother, fother,
    eacc, ebf, stage, own_sum, other_sum, sum_x, sum_z,
    lsem, sib_send, sib_recv, msend, mrecv, gsend, grecv, usend, urecv,
    asend, arecv, fsend, frecv, osem, orecv, nsem, nrecv, ssend, srecv,
):
    plane = Plane()
    y, z, x, core = plane.y, plane.z, plane.x, plane.core
    remote = plane.remote
    me = chip_of(z, x)
    own_spot = (1 - core) * (x * RING + z) + core * (z * RING + x)

    partners = [at(y, z, x + 1, core), at(y, z, x + 2, core), at(y, z, x + 3, core),
                at(y, z + 1, x, core), at(y, z + 2, x, core), at(y, z + 3, x, core),
                plane.sibling, at(ring(y, 1), z, x, core), at(ring(y, 3), z, x, core)]
    load_x = pltpu.make_async_copy(xs.at[0], xin, lsem.at[0])
    own_u = ubuf.at[:, pl.ds(multiple(me * LANE, LANE), LANE)]
    barrier = pltpu.get_barrier_semaphore()
    for partner in partners:
        pl.semaphore_signal(barrier, 1, device_id=partner, device_id_type=MESH)

    @pl.when(y == RING - 1)
    def _():
        for micro in range(2):
            pltpu.make_async_copy(
                cot.at[micro],
                ubuf.at[pl.ds(micro * LANE, LANE), pl.ds(multiple(me * LANE, LANE), LANE)],
                lsem.at[3]).start()

    load_x.start()
    own_m = mbuf.at[pl.ds(multiple(core * HALF + own_spot * LANE, LANE), LANE), :]

    def load_rows(src, at_stage, which):
        for half in (0, 1):
            pltpu.make_async_copy(src.at[0, :, pl.ds(half * HALF, HALF)],
                                  stage.at[at_stage, pl.ds(half * LANE, LANE), :], lsem.at[which]).start()

    def given(at_stage, dst, which):
        return remote(stage.at[at_stage + 1, pl.ds(0, LANE), :], dst, sib_send.at[which], sib_recv.at[which])

    def split_rows(at_stage, dst, which, own_which):
        whole = stage.at[at_stage]
        pltpu.make_async_copy(whole, whole, lsem.at[own_which]).wait()
        for k in range(CHIPS):
            half, lanes = k // 8, pl.ds(k * LANE, LANE)
            for mine in (1, 0):
                which_core = core if mine else 1 - core
                source = pl.ds(multiple((2 * (k % 8) + which_core) * LANE, LANE), LANE)
                piece = stage[at_stage, pl.ds(half * LANE, LANE), source]
                if mine:
                    dst[:, lanes] = piece
                else:
                    stage[at_stage + 1, pl.ds(0, LANE), lanes] = piece
        given(at_stage, dst, which).start()

    load_rows(m, 0, 1)
    load_rows(w, 2, 2)
    pl.semaphore_wait(barrier, len(partners))

    def u_slot(z_at, x_at, part):
        return ubuf.at[pl.ds(part * LANE, LANE), pl.ds(multiple((z_at * RING + x_at) * LANE, LANE), LANE)]

    gather_u = TwoStage(plane, u_slot, usend, urecv)

    @pl.when(y == RING - 1)
    def _():
        pltpu.make_async_copy(own_u, own_u, lsem.at[3]).wait()
        gather_u.start()

    split_rows(0, own_m, 0, 1)

    load_x.wait()
    values = xin[...].reshape(TOKENS, LANE).astype(F32)
    sigmoid_val = jax.nn.sigmoid(values)
    slope[...] = sigmoid_val * (1.0 + values * (1.0 - sigmoid_val))
    gated = (values * sigmoid_val).astype(BF).astype(F32)
    gbuf[core, pl.ds(multiple(own_spot * LANE, LANE), LANE), :] = jnp.transpose(gated).astype(BF)

    def load_weights():
        split_rows(2, wbuf.at[core], 1, 2)

    def g_slot(z_at, x_at, part):
        spot = (1 - core) * (x_at * RING + z_at) + core * (z_at * RING + x_at)
        return gbuf.at[core, pl.ds(multiple(spot * LANE + part * 64, 64), 64), :]

    bulk = Bulk(plane, mbuf, msend, mrecv)
    gather_g = TwoStage(plane, g_slot, gsend, grecv)

    def from_above():
        return remote(dbuf, own_u, sib_send.at[3], sib_recv.at[3], at(ring(y, 3), z, x, core))

    def own_rows_here():
        given(0, own_m, 0).wait()

    def go(number):
        taken = [at_y for at_y, rounds in EXTRA.items() if number in rounds]
        if not taken:
            bulk.round(number)
        else:
            @pl.when(y != taken[0])
            def _():
                bulk.round(number)

    def chain():
        @pl.when(y < RING - 1)
        def _():
            from_above().wait_recv()
            gather_u.start()

        gather_u.forward()
        for at_y, rounds in EXTRA.items():
            @pl.when(y == at_y)
            def _(rounds=rounds, at_y=at_y):
                if at_y == RING - 1:
                    gather_g.start()
                    own_rows_here()
                    load_weights()
                for number in rounds:
                    bulk.round(number)

        gather_u.finish()

        @pl.when(y > 0)
        def _():
            back_product()

    def back_product():
        given(2, wbuf.at[core], 1).wait()
        full = ubuf[...]
        bsend[...] = lax.dot_general(full, wbuf[1 - core], NT, preferred_element_type=F32)
        give = remote(bsend, brecv, sib_send.at[2], sib_recv.at[2])
        give.start()
        bown[...] = lax.dot_general(full, wbuf[core], NT, preferred_element_type=F32)
        give.wait()
        back = bown[...] + brecv[...]
        upstream = ubuf[:, pl.ds(multiple(me * LANE, LANE), LANE)].astype(F32)
        dbuf[...] = (upstream + slope[...] * back).astype(BF)

        @pl.when(y > 0)
        def _():
            from_above().start()

        for micro in range(2):
            pltpu.make_async_copy(
                dbuf.at[pl.ds(micro * LANE, LANE), :], dout.at[0, micro], lsem.at[4]).start()

    def front(index, carry):
        @pl.when(index == RING - 1 - y)
        def _():
            chain()

        for which, rounds in enumerate(CHUNKS):
            @pl.when(index == which)
            def _(which=which, rounds=rounds):
                if which == 0:
                    @pl.when(y < RING - 1)
                    def _():
                        gather_g.start()
                        own_rows_here()
                        load_weights()
                if which == 1:
                    gather_g.forward()
                for number in rounds:
                    go(number)
        return carry

    lax.fori_loop(0, RING, front, 0)

    def share(part):
        return remote(gbuf.at[part], gbuf.at[part], sib_send.at[4], sib_recv.at[4])

    gather_g.finish()
    share(core).start()

    share(1 - core).wait_recv()
    sums = jnp.zeros((8, LANE), F32)
    for part in (0, 1):
        one, two = plane.own(part)
        spot = one * RING + two
        grad = lax.dot_general(
            gbuf[part, pl.ds(multiple(spot * LANE, LANE), LANE), :], ubuf[...], NN,
            preferred_element_type=F32)
        old = mbuf[pl.ds(multiple(part * HALF + spot * LANE, LANE), LANE), :].astype(F32)
        fresh = (0.95 * old + grad).astype(BF)
        nrow[pl.ds(part * LANE, LANE), :] = fresh
        wide = fresh.astype(F32)
        square = wide * wide
        for k in range(CHIPS):
            sums = sums + jnp.sum(
                square[:, k * LANE:(k + 1) * LANE].reshape(16, 8, LANE), axis=0)
    own_sum[...] = sums
    swap = remote(own_sum, other_sum, sib_send.at[5], sib_recv.at[5])
    swap.start()

    def give_rows(buf, out, sem, recv, lanes=pl.ds(0, HALF)):
        pltpu.make_async_copy(
            buf.at[pl.ds(multiple(core * LANE, LANE), LANE), lanes], out.at[core, :, lanes], sem.at[0]).start()
        remote(buf.at[pl.ds(multiple((1 - core) * LANE, LANE), LANE), lanes], out.at[core, :, lanes],
               sem.at[1], recv).start()

    def wait_rows(buf, sem, recv):
        half = buf.at[pl.ds(0, LANE), :]
        pltpu.make_async_copy(half, half, sem.at[0]).wait()
        both = remote(half, half, sem.at[1], recv)
        both.wait_send()
        both.wait_recv()

    give_rows(nrow, nout, nsem, nrecv)

    def to_ring(buf, axis, steps, own):
        return remote(buf.at[own], buf.at[own], ssend.at[axis, steps - 1], srecv.at[axis, own],
                      plane.target(0, axis, steps))

    def start_ring(buf, axis, own, value):
        buf[own] = value
        for steps in (1, 2, 3):
            to_ring(buf, axis, steps, own).start()

    def wait_ring(buf, axis, own):
        for steps in (1, 2, 3):
            to_ring(buf, axis, steps, ring(own, steps)).wait_recv()
        return buf[0] + buf[1] + buf[2] + buf[3]

    def own_first(part):
        return x + part * (z - x)

    def own_second(part):
        return z + part * (x - z)

    def group_rows(index, part):
        return multiple(ring(own_first(part), offset_of(index)) * 512, 512)

    def both_parts(body):
        def one(part, carry):
            body(part)
            return carry

        lax.fori_loop(0, 2, one, 0)

    def slot_lanes(slot, width):
        return pl.ds(multiple(slot * width, width), width)

    fpart, fwhole = apart, aother

    def a_copy(slot):
        lanes = slot_lanes(slot, 512)
        return remote(apart.at[:, lanes], aother.at[:, lanes], asend.at[slot], arecv.at[slot])

    def f_copy(slot):
        lanes = slot_lanes(slot, 1024)
        return remote(fpart.at[:, lanes], fother.at[:, lanes], fsend.at[slot], frecv.at[slot])

    def build_and_gram(index):
        def body(part):
            start = group_rows(index, part)
            rows = pl.ds(multiple(part * HALF + start, 512), 512)
            grad = lax.dot_general(gbuf[part, pl.ds(start, 512), :], ubuf[...], NN,
                                   preferred_element_type=F32)
            nbuf[rows, :] = (0.95 * mbuf[rows, :].astype(F32) + grad).astype(BF)
            product = lax.dot_general(nrow[...], nbuf[rows, :], NT, preferred_element_type=F32)
            apart[:, slot_lanes(index * 2 + part, 512)] = (product * inverse).astype(BF)
            a_copy(index * 2 + part).start()

        both_parts(body)

    def cubic(index):
        def body(part):
            rows = pl.ds(multiple(part * HALF + group_rows(index, part), 512), 512)
            slot = index * 2 + part
            a_copy(slot).wait_recv()
            lanes = slot_lanes(slot, 512)
            whole = (apart[:, lanes].astype(F32) + aother[:, lanes].astype(F32)).astype(BF)
            eacc[...] += lax.dot_general(whole, nbuf[rows, :], NN, preferred_element_type=F32)

        both_parts(body)

    def small(second):
        def body(part):
            first, last = ring(own_first(part), OFFSETS[3]), ring(own_second(part), second)
            start = multiple((first * RING + last) * LANE, LANE)
            rows = pl.ds(multiple(part * HALF + start, LANE), LANE)
            grad = lax.dot_general(gbuf[part, pl.ds(start, LANE), :], ubuf[...], NN,
                                   preferred_element_type=F32)
            fresh = (0.95 * mbuf[rows, :].astype(F32) + grad).astype(BF)
            nbuf[rows, :] = fresh
            stage[second, pl.ds(multiple(part * LANE, LANE), LANE), :] = fresh

        both_parts(body)
        product = lax.dot_general(nrow[...], stage[second], NT, preferred_element_type=F32)
        lanes = slot_lanes(12 + second, ROWS)
        apart[:, lanes] = (product * inverse).astype(BF)
        small_copy(second).start()

    def small_copy(second):
        lanes = slot_lanes(12 + second, ROWS)
        return remote(apart.at[:, lanes], aother.at[:, lanes],
                      asend.at[6 + second], arecv.at[6 + second])

    def small_cubic(second):
        small_copy(second).wait_recv()
        lanes = slot_lanes(12 + second, ROWS)
        whole = (apart[:, lanes].astype(F32) + aother[:, lanes].astype(F32)).astype(BF)
        eacc[...] += lax.dot_general(whole, stage[second], NN, preferred_element_type=F32)

    def settle():
        @pl.when(y > 0)
        def _():
            from_above().wait_send()

        pltpu.make_async_copy(dbuf, dbuf, lsem.at[4]).wait()
        share(core).wait_send()
        gather_g.drain()
        gather_u.drain()
        for steps in (1, 2, 3):
            to_ring(sum_x, 0, steps, 0).wait_send()
        for slot in range(4):
            a_copy(slot).wait_send()
        small_copy(0).wait_send()
        small_copy(1).wait_send()
        wait_rows(nrow, nsem, nrecv)

    go(8)
    swap.wait()
    chip_sum = own_sum[...] + other_sum[...]
    start_ring(sum_x, 0, x, chip_sum)
    chip_norm = jnp.sqrt(jnp.maximum(jnp.sum(chip_sum), 1e-30))
    inverse = 1.0 / chip_norm
    eacc[...] = jnp.zeros_like(eacc)

    def stream(index, carry):
        @pl.when(index == 2)
        def _():
            def pieces(k, carry):
                second = offset_of(k)

                @pl.when(k == 1)
                def _():
                    bulk.wait(2, 1, 0)

                @pl.when(k == 2)
                def _():
                    bulk.wait(2, 3, 1)

                small(second)

                @pl.when(k > 0)
                def _():
                    small_cubic(offset_of(k - 1))

                return carry

            lax.fori_loop(0, 3, pieces, 0)
            settle()

        bulk.complete(offset_of(index))

        @pl.when(index == 0)
        def _():
            go(9)

        build_and_gram(index)

        @pl.when(index == 0)
        def _():
            @pl.when(y == 0)
            def _():
                back_product()

            go(10)

        @pl.when(index == 1)
        def _():
            go(12)

        cubic(index)

        @pl.when(index == 0)
        def _():
            go(11)
            start_ring(sum_z, 1, z, wait_ring(sum_x, 0, x))

        @pl.when(index == 1)
        def _():
            go(13)
            go(14)

        return carry

    lax.fori_loop(0, 3, stream, 0)
    sum_squares = jnp.sum(wait_ring(sum_z, 1, z))
    scaling = 0.4 / jnp.sqrt(float(WIDTH) * (sum_squares / float(WIDTH * WIDTH) + 1e-06))
    bulk.wait(2, 2, 0)
    bulk.wait(2, 2, 1)
    small(2)

    def last_pieces(k, carry):
        small_cubic(offset_of(k))
        return carry

    lax.fori_loop(2, 4, last_pieces, 0)
    ebf[...] = (((eacc[...] * scaling) * scaling) * (scaling * chip_norm)).astype(BF)

    for slot in (4, 5):
        a_copy(slot).wait_send()
    small_copy(2).wait_send()
    small_copy(3).wait_send()
    obuf = stage.at[0]

    def all_back(slot, carry):
        product = lax.dot_general(ebf[...], nbuf[pl.ds(multiple(slot * 1024, 1024), 1024), :], NT,
                                  preferred_element_type=F32)
        fpart[:, slot_lanes(slot, 1024)] = (product * scaling).astype(BF)
        f_copy(slot).start()
        return carry

    lax.fori_loop(0, 4, all_back, 0)

    def back_whole(slot):
        f_copy(slot).wait_recv()
        lanes = slot_lanes(slot, 1024)
        fwhole[:, lanes] = (fpart[:, lanes].astype(F32) + fother[:, lanes].astype(F32)).astype(BF)

    for slot in range(3):
        back_whole(slot)

    def cuts(cut, carry):
        lanes = pl.ds(multiple(cut * 512, 512), 512)
        product = lax.dot_general(fwhole[:, pl.ds(0, 3072)], nbuf[pl.ds(0, 3072), lanes], NN,
                                  preferred_element_type=F32)

        @pl.when(cut == 0)
        def _():
            back_whole(3)

        product = product + lax.dot_general(
            fwhole[:, pl.ds(3072, 1024)], nbuf[pl.ds(3072, 1024), lanes], NN, preferred_element_type=F32)
        scaled = (nrow[:, lanes].astype(F32) * scaling).astype(BF).astype(F32)
        mixed = (quintic_a * scaled + quintic_b * ebf[:, lanes].astype(F32)
                 + quintic_c * (product * scaling))
        obuf[:, lanes] = (math.sqrt(WIDTH) * mixed).astype(BF)
        give_rows(obuf, oout, osem, orecv, lanes)
        return carry

    lax.fori_loop(0, 4, cuts, 0)

    for steps in (1, 2, 3):
        to_ring(sum_z, 1, steps, 0).wait_send()
    for number in range(15 - DEPTH, 15):
        bulk.sent(number)
    for slot in range(4):
        f_copy(slot).wait_send()
    wait_rows(obuf, osem, orecv)


def copy_kernel(grads, fresh, update, grads_out, fresh_out, update_out, small, halves, wholes, come, leave):
    grads_in = pltpu.make_async_copy(grads, small, come.at[4])
    grads_away = pltpu.make_async_copy(small, grads_out, leave.at[4])
    arriving, leaving = [], []
    for which, (src, dst) in enumerate(((fresh, fresh_out), (update, update_out))):
        for k in range(2):
            rows, number = pl.ds(k * 64, 64), which * 2 + k
            arriving.append(pltpu.make_async_copy(src.at[:, rows], halves.at[number], come.at[number]))
            leaving.append(pltpu.make_async_copy(wholes.at[number], dst.at[0, rows], leave.at[number]))
    for one in arriving:
        one.start()
    grads_in.start()
    for number in range(4):
        arriving[number].wait()
        for k in range(CHIPS):
            for half in range(2):
                wholes[number, :, (2 * k + half) * LANE:(2 * k + half + 1) * LANE] = (
                    halves[number, half, :, k * LANE:(k + 1) * LANE])
        leaving[number].start()
    grads_in.wait()
    grads_away.start()
    for one in leaving:
        one.wait()
    grads_away.wait()


def per_device(cotangent, stashed_inputs, weights, momentum):
    anywhere = pl.BlockSpec(memory_space=pl.ANY)
    sem = pltpu.SemaphoreType.DMA
    scratch = [
        pltpu.VMEM((WIDTH, HALF), BF),
        pltpu.VMEM((WIDTH, HALF), BF),
        pltpu.VMEM((ROWS, HALF), BF),
        pltpu.VMEM((2, LANE, HALF), BF),
        pltpu.VMEM((TOKENS, HALF), BF),
        pltpu.VMEM((2, HALF, TOKENS), BF),
        pltpu.VMEM((2, LANE, LANE), BF),
        pltpu.VMEM((TOKENS, LANE), F32),
        pltpu.VMEM((TOKENS, LANE), BF),
        pltpu.VMEM((TOKENS, LANE), F32),
        pltpu.VMEM((TOKENS, LANE), F32),
        pltpu.VMEM((TOKENS, LANE), F32),
        pltpu.VMEM((ROWS, WIDTH), BF),
        pltpu.VMEM((ROWS, WIDTH), BF),
        pltpu.VMEM((ROWS, WIDTH), BF),
        pltpu.VMEM((ROWS, HALF), F32),
        pltpu.VMEM((ROWS, HALF), BF),
        pltpu.VMEM((RING, ROWS, HALF), BF),
        pltpu.VMEM((8, LANE), F32),
        pltpu.VMEM((8, LANE), F32),
        pltpu.VMEM((RING, 8, LANE), F32),
        pltpu.VMEM((RING, 8, LANE), F32),
        sem((5,)),
        sem((6,)),
        sem((6,)),
        sem((60,)),
        sem((2, CHIPS, 2)),
        sem((30,)),
        sem((2, CHIPS)),
        sem((30,)),
        sem((2, CHIPS)),
        sem((10,)),
        sem((10,)),
        sem((4,)),
        sem((4,)),
        sem((2,)),
        sem,
        sem((2,)),
        sem,
        sem((2, 3)),
        sem((2, RING)),
    ]
    held = pl.pallas_call(
        step_kernel,
        out_shape=(
            jax.ShapeDtypeStruct(stashed_inputs.shape, BF),
            jax.ShapeDtypeStruct((2, LANE, HALF), BF),
            jax.ShapeDtypeStruct((2, LANE, HALF), BF),
        ),
        in_specs=[anywhere] * 4,
        out_specs=(anywhere, anywhere, anywhere),
        scratch_shapes=scratch,
        compiler_params=pltpu.CompilerParams(
            collective_id=0, has_side_effects=True, vmem_limit_bytes=62 * 1024 * 1024),
        cost_estimate=pl.CostEstimate(
            flops=22 * 10**9, bytes_accessed=6 * 2**20, transcendentals=32768),
    )(cotangent, stashed_inputs, weights, momentum)
    return pl.pallas_call(
        copy_kernel,
        out_shape=(
            jax.ShapeDtypeStruct(stashed_inputs.shape, BF),
            jax.ShapeDtypeStruct(momentum.shape, BF),
            jax.ShapeDtypeStruct(momentum.shape, BF),
        ),
        in_specs=[anywhere] * 3,
        out_specs=(anywhere, anywhere, anywhere),
        scratch_shapes=[
            pltpu.VMEM((1, 2, LANE, LANE), BF), pltpu.VMEM((4, 2, 64, HALF), BF),
            pltpu.VMEM((4, 64, WIDTH), BF), sem((5,)), sem((5,))],
    )(*held)


def solution(mesh):
    in_specs = (
        P(None, None, "dp"),
        P("pipe", None, None, "dp"),
        P("pipe", "dp", None),
        P("pipe", "dp", None),
    )
    out_specs = (P("pipe", None, None, "dp"), P("pipe", "dp", None), P("pipe", "dp", None))
    return jax.shard_map(
        per_device, mesh=mesh, in_specs=in_specs, out_specs=out_specs, check_vma=False
    )
```
